128 devices in a mesh: prow: 16 (over x, y), pcol: 8 (over z, core).
Axes of the slice: x: 4, y: 4, z: 4, core: 2. Of those that a mesh axis runs over, the one named last changes fastest.
Arguments:
- matrix: float32 [16384, 16384], P('prow', 'pcol'), may hold values from -17 to 17
- pivots: int32 [128], replicated, may hold values from 0 to 16383, as said below
Outputs:
- updated: float32 [16384, 16384], P('prow', 'pcol')
The draws below stay inside these ranges and needn't reach their ends.
Inputs may be any that keep to these rules, and one draw needn't show every extreme that they name: `pivots`: entry j lies between j and 16383; one entry equals 16383.
All inputs are finite; a program needn't handle non-finite values.
Results may differ from the reference program's by a relative error of at most 0.000075.
Values sent between devices are 32-bit elements; how exact they have to be, the bound alone decides.
A program may use at most 64 MiB of HBM per device.

```python
import math
import jax
import jax.numpy as jnp
from jax import lax

NB = 128
M = 16384


def draw_matrix(key, part):
    key = jax.random.fold_in(key, 1)
    first_key = jax.random.fold_in(key, 0)
    values = jnp.clip(jax.random.normal(first_key, (M, M), jnp.float32), -6.0, 6.0)
    rows = jnp.arange(M, dtype=jnp.int32)[:, None]
    columns = jnp.arange(M, dtype=jnp.int32)[None, :]
    panel_values = jnp.clip(values, -1.7, 1.7)
    factor = jnp.where(rows < NB, 0.5, 1.0) / math.sqrt(NB)
    return jnp.where(columns < NB, panel_values * factor, values)


def draw_pivots(key, part):
    key = jax.random.fold_in(key, 2)
    first_key, second_key = jax.random.split(key)
    steps = jnp.arange(NB, dtype=jnp.int32)
    offsets = jax.random.randint(first_key, (NB,), 0, M, dtype=jnp.int32)
    chosen = steps + offsets % (M - steps)
    which = jax.random.randint(second_key, (), 0, NB, dtype=jnp.int32)
    return jnp.where(steps == which, M - 1, chosen).astype(jnp.int32)


def setup_inputs(seed: int = 0) -> dict:
    streams_of = jax.random.split(jax.random.key(seed), 3)
    matrix = draw_matrix(jax.random.fold_in(streams_of[2], 71), 0)
    pivots = draw_pivots(jax.random.fold_in(streams_of[2], 71), 0)
    return {"matrix": matrix, "pivots": pivots}


def reference(matrix, pivots):

    def swap_rows(j, arrangement):
        first = arrangement[j]
        second = arrangement[pivots[j]]
        return arrangement.at[j].set(second).at[pivots[j]].set(first)
    arrangement = lax.fori_loop(0, NB, swap_rows, jnp.arange(M, dtype=jnp.int32))
    places = jnp.concatenate([jnp.arange(NB, dtype=jnp.int32), pivots.astype(jnp.int32)])
    swapped = matrix.at[places].set(matrix[arrangement[places]])
    top_rows = swapped[:NB]
    diag_part = jnp.tril(matrix[:NB, :NB], -1) + jnp.eye(NB, dtype=jnp.float32)
    upper_rows = jax.scipy.linalg.solve_triangular(diag_part, top_rows, lower=True, unit_diagonal=True)
    rest = swapped[NB:] - jnp.dot(matrix[NB:, :NB].astype(jnp.float32), upper_rows.astype(jnp.float32), precision=lax.Precision.HIGHEST, preferred_element_type=jnp.float32)
    result = jnp.concatenate([upper_rows, rest], axis=0)
    columns = jnp.arange(M, dtype=jnp.int32)
    return jnp.where(columns[None, :] >= NB, result, matrix)
```

```python
import functools

import jax
import jax.numpy as jnp
from jax import lax
from jax.experimental import pallas as pl
from jax.experimental.pallas import tpu as pltpu
from jax.sharding import PartitionSpec as P

NB = 128
PROWS = 16
SIDE = 4
FEW = 24
VMEM_BYTES = 60 * 1024 * 1024
HIGHEST = lax.Precision.HIGHEST


def plan_kernel(
    pivots, matrix, picks, owner, slot, leaving, place, info, arrangement, count, sems
):
    rows_dev = matrix.shape[0]
    me = lax.axis_index("prow")

    def start_top(j, carry):
        arrangement[j] = j
        return carry

    def start_pivot(j, carry):
        p = pivots[j]
        arrangement[p] = p
        return carry

    def start_count(r, carry):
        count[r] = 0
        return carry

    lax.fori_loop(0, NB, start_top, 0, unroll=8)
    lax.fori_loop(0, NB, start_pivot, 0, unroll=8)
    lax.fori_loop(0, PROWS, start_count, 0, unroll=8)

    def row_copy(source, s):
        return pltpu.make_async_copy(
            matrix.at[pl.ds(source, 1), :], picks.at[pl.ds(s, 1), :], sems.at[s]
        )

    def interchange(j, carry):
        p = pivots[j]
        first = arrangement[j]
        second = arrangement[p]
        arrangement[j] = second
        arrangement[p] = first
        r = second // rows_dev
        s = count[r]
        count[r] = s + 1
        owner[j] = r
        slot[j] = s

        @pl.when(r == me)
        def _():
            source = second - r * rows_dev
            row_copy(source, s).start()
            place[s] = jnp.where(second >= NB, source, -1)

        return carry

    lax.fori_loop(0, NB, interchange, 0, unroll=4)

    def leave(j, carry):
        leaving[owner[j] * NB + slot[j]] = arrangement[arrangement[j]]
        return carry

    lax.fori_loop(0, NB, leave, 0, unroll=4)

    def most(r, carry):
        return jnp.maximum(carry, count[r])

    info[0] = count[me]
    info[1] = lax.fori_loop(0, PROWS, most, 0, unroll=8)

    def finish(s, carry):
        row_copy(0, s).wait()
        return carry

    lax.fori_loop(0, count[me], finish, 0)


def invert_unit_lower(block):
    rows = lax.broadcasted_iota(jnp.int32, (NB, NB), 0)
    cols = lax.broadcasted_iota(jnp.int32, (NB, NB), 1)
    eye = jnp.where(rows == cols, 1.0, 0.0).astype(jnp.float32)
    dot = functools.partial(jnp.dot, precision=HIGHEST, preferred_element_type=jnp.float32)
    inverse = eye
    size = 1
    while size < NB:
        corner = (rows // size == cols // size + 1) & (rows // (2 * size) == cols // (2 * size))
        part = jnp.where(corner, block, 0.0)
        if size == 1:
            inverse = eye - part
        else:
            inverse = inverse - dot(dot(inverse, part), inverse)
        size *= 2
    return inverse


def exchange_kernel(
    slots,
    owner, slot, leaving, matrix, picks,
    gathered, panel, inverse, returned,
    received, ordered, top, top_a, top_b, back, corner,
    row_send, row_recv, ret_send, ret_recv, ring_send, ring_recv,
    top_send, top_recv, panel_send, panel_recv, inv_send, inv_recv, own_sem,
):
    half, quarter = NB // 2, NB // 4
    rows_dev = matrix.shape[0]
    me = lax.axis_index("prow")
    col = lax.axis_index("pcol")
    x, y = me // SIDE, me % SIDE
    z, core = col // 2, col % 2
    sent = []

    def block(q):
        return pl.ds(pl.multiple_of(q * NB, NB), NB)

    def remote(src, dst, send_sem, recv_sem, device):
        return pltpu.make_async_remote_copy(
            src_ref=src, dst_ref=dst, send_sem=send_sem, recv_sem=recv_sem, device_id=device
        )

    z_up, z_down = ((z + 1) % 4) * 2 + core, ((z + 3) % 4) * 2 + core
    other = z * 2 + 1 - core
    barrier = pltpu.get_barrier_semaphore()
    for d in range(1, PROWS):
        pl.semaphore_signal(barrier, inc=1, device_id={"prow": (me + d) % PROWS})
    for c in (z_up, z_down, other):
        pl.semaphore_signal(barrier, inc=1, device_id={"pcol": c})

    own_rows = pltpu.make_async_copy(
        picks.at[pl.ds(0, slots), block(me)],
        received.at[pl.ds(pl.multiple_of(me * slots, 8), slots)],
        own_sem.at[0],
    )
    own_rows.start()
    pl.semaphore_wait(barrier, PROWS - 1 + 3)

    def row_copy(d):
        peer = (me + d) % PROWS
        return remote(
            picks.at[pl.ds(0, slots), block(peer)],
            received.at[pl.ds(pl.multiple_of(me * slots, 8), slots)],
            row_send.at[d], row_recv.at[d], {"prow": peer},
        )

    def row_start(d, carry):
        row_copy(d).start()
        return carry

    def row_wait(d, carry):
        row_copy(d).wait_recv()
        return carry

    def row_sent(d, carry):
        row_copy(d).wait_send()
        return carry

    lax.fori_loop(1, PROWS, row_start, 0)

    def top_x(d):
        return remote(
            matrix.at[pl.ds(0, half), pl.ds(d * SIDE * NB, SIDE * NB)], top_a,
            top_send.at[d], top_recv.at[0], {"prow": d * SIDE},
        )

    def top_y(d, k):
        return remote(
            matrix.at[pl.ds(half, half), pl.ds((k * SIDE + d) * NB, NB)],
            top_b.at[:, pl.ds(k * NB, NB)],
            top_send.at[4 + 4 * d + k], top_recv.at[1 + k], {"prow": d},
        )

    top_own = [
        pltpu.make_async_copy(
            matrix.at[pl.ds(0, half), pl.ds(0, SIDE * NB)], top_a, own_sem.at[1]
        )
    ] + [
        pltpu.make_async_copy(
            matrix.at[pl.ds(half, half), pl.ds(k * SIDE * NB, NB)],
            top_b.at[:, pl.ds(k * NB, NB)], own_sem.at[2 + k],
        )
        for k in range(SIDE)
    ]
    diagonal = pltpu.make_async_copy(matrix.at[pl.ds(0, NB), pl.ds(0, NB)], corner, own_sem.at[6])

    @pl.when(me == 0)
    def _():
        for d in (1, 3, 2):
            top_x(d).start()
            for k in range(SIDE):
                top_y(d, k).start()
        for c in top_own:
            c.start()

    halves = [pl.ds(0, rows_dev // 2), pl.ds(rows_dev // 2, rows_dev // 2)]
    first_panel = matrix.at[:, pl.ds(0, NB)]

    def panel_first(h, k, to):
        return remote(
            first_panel.at[halves[h]], panel.at[halves[h]],
            panel_send.at[k], panel_recv.at[h], {"pcol": to},
        )

    def panel_next(h, k, to):
        return remote(
            panel.at[halves[h]], panel.at[halves[h]],
            panel_send.at[k], panel_recv.at[h], {"pcol": to},
        )

    panel_own = pltpu.make_async_copy(first_panel, panel, own_sem.at[7])

    @pl.when(col == 0)
    def _():
        panel_first(0, 0, z_up).start()
        panel_first(1, 1, z_down).start()
        panel_first(1, 2, z_up).start()
        panel_first(0, 3, z_down).start()
        panel_first(0, 4, other).start()
        panel_first(1, 5, other).start()
        panel_own.start()

    @pl.when((me == 0) & (col == 0))
    def _():
        diagonal.start()
        diagonal.wait()
        inverse[...] = invert_unit_lower(corner[...])

    own_rows.wait()
    lax.fori_loop(1, PROWS, row_wait, 0)

    def order(j, carry):
        ordered[pl.ds(j, 1), :] = received[pl.ds(owner[j] * slots + slot[j], 1), :]
        return carry

    lax.fori_loop(0, NB, order, 0, unroll=8)
    gathered[:, block(me)] = ordered[...]

    def at(xx, yy):
        return ((xx + 2 * SIDE) % SIDE) * SIDE + (yy + 2 * SIDE) % SIDE

    class Ring:
        def __init__(self, o):
            self.o = o
            self.row0 = o * half

        def where(self, along, across):
            return at(x + along, y + across) if self.o == 0 else at(x + across, y + along)

        def device(self, along, across):
            return {"prow": self.where(along, across)}

        def copy(self, q, part, sem, device):
            start, size = ((0, half), (0, quarter), (quarter, quarter))[part]
            ref = gathered.at[pl.ds(self.row0 + start, size), block(q)]
            return remote(ref, ref, ring_send.at[self.o, sem], ring_recv.at[self.o, sem], device)

        def send(self, q, part, sem, device):
            c = self.copy(q, part, sem, device)
            c.start()
            sent.append(c)

        def wait(self, q, part, sem):
            self.copy(q, part, sem, self.device(0, 1)).wait_recv()

    rings = (Ring(0), Ring(1))
    steps = (0, -1, 1, 2)

    def first_own(ring):
        q = ring.where(0, 0)
        ring.send(q, 0, 0, ring.device(1, 0))
        ring.send(q, 0, 1, ring.device(-1, 0))

    def second(ring, i):
        q = ring.where(steps[i], 0)
        ring.send(q, 0, 4 + 4 * i, ring.device(0, 1))
        ring.send(q, 0, 5 + 4 * i, ring.device(0, -1))

    def first_near(ring, i):
        q = ring.where(steps[i], 0)
        ring.wait(q, 0, i - 1)
        ring.send(q, i, 1 + i, ring.device(-steps[i], 0))

    def first_far(ring):
        q = ring.where(2, 0)
        ring.wait(q, 1, 2)
        ring.wait(q, 2, 3)

    def second_near(ring, i):
        for n, (step, part) in enumerate(((-1, 1), (1, 2))):
            q = ring.where(steps[i], step)
            ring.wait(q, 0, 4 + 4 * i + n)
            ring.send(q, part, 6 + 4 * i + n, ring.device(0, -step))

    def second_far(ring, i):
        q = ring.where(steps[i], 2)
        ring.wait(q, 1, 6 + 4 * i)
        ring.wait(q, 2, 7 + 4 * i)

    for ring in rings:
        first_own(ring)
    for ring in rings:
        second(ring, 0)
    for i in (1, 2):
        for ring in rings:
            first_near(ring, i)
            second(ring, i)

    def top_leg(a, d):
        if a == 0:
            src, dst, device = top_a, top.at[pl.ds(0, half)], x * SIDE + d
        else:
            src, dst, device = top_b, top.at[pl.ds(half, half)], d * SIDE + y
        return remote(
            src.at[:, pl.ds(d * NB, NB)], dst,
            top_send.at[20 + 4 * a + d], top_recv.at[5 + a], {"prow": device},
        )

    @pl.when(me == 0)
    def _():
        for c in top_own:
            c.wait()

    @pl.when(y == 0)
    def _():
        @pl.when(x != 0)
        def _():
            top_x(1).wait_recv()

        for d in range(1, SIDE):
            top_leg(0, d).start()
        top[pl.ds(0, half), :] = top_a[:, pl.ds(0, NB)]

    @pl.when(x == 0)
    def _():
        @pl.when(y != 0)
        def _():
            for k in range(SIDE):
                top_y(1, k).wait_recv()

        for d in range(1, SIDE):
            top_leg(1, d).start()
        top[pl.ds(half, half), :] = top_b[:, pl.ds(0, NB)]

    for ring in rings:
        first_far(ring)
        second(ring, 3)
    for ring in rings:
        second_near(ring, 0)

    def panel_leg(h):
        @pl.when((core == 0) & (z > 0))
        def _():
            panel_next(h, 0, other).wait_recv()
            panel_next(h, 4 + h, other).start()

            @pl.when((z == 1) if h == 0 else (z == 3))
            def _():
                panel_next(h, 0, 4).start()

    panel_leg(0)
    panel_leg(1)

    @pl.when(y != 0)
    def _():
        top_leg(0, 1).wait_recv()

    @pl.when(x != 0)
    def _():
        top_leg(1, 1).wait_recv()

    def back_rows(r, carry):
        for s in range(slots):
            index = leaving[r * NB + s] & (NB - 1)
            back[pl.ds(r * slots + s, 1), :] = top[pl.ds(index, 1), :]
        return carry

    lax.fori_loop(0, PROWS, back_rows, 0)

    def ret_copy(d):
        peer = (me + d) % PROWS
        return remote(
            back.at[pl.ds(pl.multiple_of(peer * slots, 8), slots)],
            returned.at[pl.ds(0, slots), block(me)],
            ret_send.at[d], ret_recv.at[d], {"prow": peer},
        )

    def ret_start(d, carry):
        ret_copy(d).start()
        return carry

    def ret_wait(d, carry):
        peer = (me - d + PROWS) % PROWS
        remote(
            back.at[pl.ds(0, slots)], returned.at[pl.ds(0, slots), block(peer)],
            ret_send.at[d], ret_recv.at[d], {"prow": peer},
        ).wait_recv()
        return carry

    def ret_sent(d, carry):
        ret_copy(d).wait_send()
        return carry

    lax.fori_loop(1, PROWS, ret_start, 0)
    ret_own = pltpu.make_async_copy(
        back.at[pl.ds(pl.multiple_of(me * slots, 8), slots)],
        returned.at[pl.ds(0, slots), block(me)], own_sem.at[8],
    )
    ret_own.start()

    for i in (1, 2, 3):
        for ring in rings:
            second_near(ring, i)

    def inv_copy(k, device):
        return remote(inverse, inverse, inv_send.at[k], inv_recv.at[0], device)

    @pl.when(col == 0)
    def _():
        @pl.when(me != 0)
        def _():
            inv_copy(0, {"pcol": other}).wait_recv()

        @pl.when(me == 0)
        def _():
            for d in range(1, SIDE):
                inv_copy(d, {"prow": d * SIDE}).start()

        @pl.when(y == 0)
        def _():
            for d in range(1, SIDE):
                inv_copy(3 + d, {"prow": x * SIDE + d}).start()

        inv_copy(7, {"pcol": z_up}).start()
        inv_copy(8, {"pcol": z_down}).start()
        inv_copy(9, {"pcol": other}).start()

    @pl.when(col != 0)
    def _():
        inv_copy(0, {"pcol": other}).wait_recv()

        @pl.when(core == 0)
        def _():
            inv_copy(9, {"pcol": other}).start()

            @pl.when(z == 1)
            def _():
                inv_copy(7, {"pcol": 4}).start()

    for i in range(4):
        for ring in rings:
            second_far(ring, i)
    lax.fori_loop(1, PROWS, ret_wait, 0)
    ret_own.wait()

    @pl.when(core == 1)
    def _():
        panel_next(0, 0, other).wait_recv()
        panel_next(1, 0, other).wait_recv()

    for c in sent:
        c.wait_send()
    lax.fori_loop(1, PROWS, row_sent, 0)
    lax.fori_loop(1, PROWS, ret_sent, 0)

    @pl.when(me == 0)
    def _():
        for d in (1, 3, 2):
            top_x(d).wait_send()
            for k in range(SIDE):
                top_y(d, k).wait_send()

    @pl.when(y == 0)
    def _():
        for d in range(1, SIDE):
            top_leg(0, d).wait_send()

    @pl.when(x == 0)
    def _():
        for d in range(1, SIDE):
            top_leg(1, d).wait_send()

    @pl.when(col == 0)
    def _():
        panel_own.wait()
        for h, k in ((0, 0), (1, 1), (1, 2), (0, 3), (0, 4), (1, 5)):
            panel_first(h, k, other).wait_send()

        @pl.when(me == 0)
        def _():
            for d in range(1, SIDE):
                inv_copy(d, {"prow": d * SIDE}).wait_send()

        @pl.when(y == 0)
        def _():
            for d in range(1, SIDE):
                inv_copy(3 + d, {"prow": x * SIDE + d}).wait_send()

        for k in (7, 8, 9):
            inv_copy(k, {"pcol": other}).wait_send()

    @pl.when((core == 0) & (z > 0))
    def _():
        panel_next(0, 4, other).wait_send()
        panel_next(1, 5, other).wait_send()
        inv_copy(9, {"pcol": other}).wait_send()

        @pl.when(z == 1)
        def _():
            panel_next(0, 0, other).wait_send()
            inv_copy(7, {"pcol": other}).wait_send()

        @pl.when(z == 3)
        def _():
            panel_next(1, 0, other).wait_send()


def exchange(slots, collective_id, owner, slot, leaving, matrix, picks):
    rows_dev, cols_dev = matrix.shape
    f32 = jnp.float32
    smem = pl.BlockSpec(memory_space=pltpu.SMEM)
    vmem = pl.BlockSpec(memory_space=pltpu.VMEM)
    anywhere = pl.BlockSpec(memory_space=pl.ANY)
    dma = pltpu.SemaphoreType.DMA
    return pl.pallas_call(
        functools.partial(exchange_kernel, slots),
        out_shape=[
            jax.ShapeDtypeStruct((NB, cols_dev), f32),
            jax.ShapeDtypeStruct((rows_dev, NB), f32),
            jax.ShapeDtypeStruct((NB, NB), f32),
            jax.ShapeDtypeStruct((NB, cols_dev), f32),
        ],
        in_specs=[smem, smem, smem, anywhere, anywhere],
        out_specs=[vmem, vmem, vmem, anywhere],
        scratch_shapes=[
            pltpu.VMEM((PROWS * slots, NB), f32),
            pltpu.VMEM((NB, NB), f32),
            pltpu.VMEM((NB, NB), f32),
            pltpu.VMEM((NB // 2, SIDE * NB), f32),
            pltpu.VMEM((NB // 2, SIDE * NB), f32),
            pltpu.VMEM((PROWS * slots, NB), f32),
            pltpu.VMEM((NB, NB), f32),
            dma((PROWS,)), dma((PROWS,)), dma((PROWS,)), dma((PROWS,)),
            dma((2, 20)), dma((2, 20)),
            dma((28,)), dma((7,)), dma((6,)), dma((2,)), dma((10,)), dma((1,)), dma((9,)),
        ],
        compiler_params=pltpu.CompilerParams(
            collective_id=collective_id, has_side_effects=True, vmem_limit_bytes=VMEM_BYTES
        ),
        name="exchange_%d" % slots,
    )(owner, slot, leaving, matrix, picks)


def split(value):
    high = value.astype(jnp.bfloat16)
    return high, (value - high.astype(jnp.float32)).astype(jnp.bfloat16)


def update_kernel(
    place, info, matrix, gathered, panel, inverse, returned, out,
    factor, chosen, chosen_factor, fixed,
):
    rows_dev = matrix.shape[0]
    step = pl.program_id(0)
    me = lax.axis_index("prow")
    col = lax.axis_index("pcol")
    owned = info[0]

    def stacked(value):
        high, low = split(value)
        return jnp.concatenate([high, low, high], axis=1)

    @pl.when(step == 0)
    def _():
        factor[...] = stacked(panel[...])

        def choose(s, carry):
            p = jnp.maximum(place[s], 0)
            chosen[pl.ds(s, 1), :] = panel[pl.ds(p, 1), :]
            return carry

        lax.fori_loop(0, owned, choose, 0)
        chosen_factor[...] = stacked(chosen[...])

    upper = jnp.dot(
        inverse[...], gathered[...], precision=HIGHEST, preferred_element_type=jnp.float32
    )
    high, low = split(upper)
    terms = jnp.concatenate([high, high, low], axis=0)
    out[...] = matrix[...] - jnp.dot(factor[...], terms, preferred_element_type=jnp.float32)

    def put(size):
        fixed[pl.ds(0, size), :] = returned[pl.ds(0, size), :] - jnp.dot(
            chosen_factor[pl.ds(0, size), :], terms, preferred_element_type=jnp.float32
        )

    @pl.when(owned <= 32)
    def _():
        put(32)

    @pl.when(owned > 32)
    def _():
        put(NB)

    def fix(s, carry):
        @pl.when(place[s] >= 0)
        def _():
            out[pl.ds(place[s], 1), :] = fixed[pl.ds(s, 1), :]

        return carry

    lax.fori_loop(0, owned, fix, 0)

    @pl.when(me == 0)
    def _():
        out[pl.ds(0, NB), :] = upper

    @pl.when((col == 0) & (step == 0))
    def _():
        out[:, pl.ds(0, NB)] = matrix[:, pl.ds(0, NB)]


def update(place, info, matrix, gathered, panel, inverse, returned):
    rows_dev, cols_dev = matrix.shape
    wide = 256
    smem = pl.BlockSpec(memory_space=pltpu.SMEM)

    def columns(rows):
        return pl.BlockSpec((rows, wide), lambda i: (0, i))

    def whole(rows):
        return pl.BlockSpec((rows, NB), lambda i: (0, 0))

    return pl.pallas_call(
        update_kernel,
        grid=(cols_dev // wide,),
        out_shape=jax.ShapeDtypeStruct(matrix.shape, jnp.float32),
        in_specs=[
            smem, smem, columns(rows_dev), columns(NB), whole(rows_dev), whole(NB), columns(NB)
        ],
        out_specs=columns(rows_dev),
        scratch_shapes=[
            pltpu.VMEM((rows_dev, 3 * NB), jnp.bfloat16),
            pltpu.VMEM((NB, NB), jnp.float32),
            pltpu.VMEM((NB, 3 * NB), jnp.bfloat16),
            pltpu.VMEM((NB, wide), jnp.float32),
        ],
        compiler_params=pltpu.CompilerParams(vmem_limit_bytes=VMEM_BYTES),
        name="update",
    )(place, info, matrix, gathered, panel, inverse, returned)


def plan(matrix, pivots):
    i32 = jnp.int32
    smem = pl.BlockSpec(memory_space=pltpu.SMEM)
    anywhere = pl.BlockSpec(memory_space=pl.ANY)
    return pl.pallas_call(
        plan_kernel,
        out_shape=[
            jax.ShapeDtypeStruct((NB, matrix.shape[1]), jnp.float32),
            jax.ShapeDtypeStruct((NB,), i32),
            jax.ShapeDtypeStruct((NB,), i32),
            jax.ShapeDtypeStruct((PROWS * NB,), i32),
            jax.ShapeDtypeStruct((NB,), i32),
            jax.ShapeDtypeStruct((8,), i32),
        ],
        in_specs=[smem, anywhere],
        out_specs=[anywhere, smem, smem, smem, smem, smem],
        scratch_shapes=[
            pltpu.SMEM((PROWS * matrix.shape[0],), i32),
            pltpu.SMEM((PROWS,), i32),
            pltpu.SemaphoreType.DMA((NB,)),
        ],
        compiler_params=pltpu.CompilerParams(vmem_limit_bytes=VMEM_BYTES),
        name="plan",
    )(pivots, matrix)


def local(matrix, pivots):
    picks, owner, slot, leaving, place, info = plan(matrix, pivots)
    gathered, panel, inverse, returned = lax.cond(
        info[1] <= FEW,
        functools.partial(exchange, FEW, 0),
        functools.partial(exchange, NB, 1),
        owner, slot, leaving, matrix, picks,
    )
    return update(place, info, matrix, gathered, panel, inverse, returned)


def solution(mesh):
    placed = (P("prow", "pcol"), P())
    return jax.shard_map(
        local, mesh=mesh, in_specs=placed, out_specs=P("prow", "pcol"), check_vma=False
    )
```

```python
import functools

import jax
import jax.numpy as jnp
from jax import lax
from jax.experimental import pallas as pl
from jax.experimental.pallas import tpu as pltpu
from jax.sharding import PartitionSpec as P

NB = 128
PROWS = 16
SIDE = 4
FEW = 24
MIB = 1024 * 1024
LOADS = 8
WIDE = 256
HIGHEST = lax.Precision.HIGHEST


def invert_unit_lower(block):
    rows = lax.broadcasted_iota(jnp.int32, (NB, NB), 0)
    cols = lax.broadcasted_iota(jnp.int32, (NB, NB), 1)
    eye = jnp.where(rows == cols, 1.0, 0.0).astype(jnp.float32)
    dot = functools.partial(jnp.dot, precision=HIGHEST, preferred_element_type=jnp.float32)
    inverse = eye
    size = 1
    while size < NB:
        corner = (rows // size == cols // size + 1) & (rows // (2 * size) == cols // (2 * size))
        part = jnp.where(corner, block, 0.0)
        if size == 1:
            inverse = eye - part
        else:
            inverse = inverse - dot(dot(inverse, part), inverse)
        size *= 2
    return inverse


def swap_plan(slots, pivots, me, rows_dev, table):
    shape = (NB, NB)
    down = lax.broadcasted_iota(jnp.int32, shape, 0)
    over = lax.broadcasted_iota(jnp.int32, shape, 1)
    earlier = over < down

    def as_row(column):
        return jnp.sum(jnp.where(down == over, column, 0), axis=0, keepdims=True)

    def as_column(row):
        return jnp.sum(jnp.where(down == over, row, 0), axis=1, keepdims=True)

    def look_up(row, index):
        return jnp.sum(jnp.where(over == index, row, 0), axis=1, keepdims=True)

    def last(where):
        return jnp.max(jnp.where(where, over, -1), axis=1, keepdims=True)

    p_row = pivots[...]
    p_col = as_column(p_row)
    steps = lax.broadcasted_iota(jnp.int32, (NB, 1), 0)
    touched = last((p_row == down) & earlier)
    held = jnp.where(touched >= 0, touched, steps)
    for _ in range(7):
        held = look_up(as_row(held), held)
    held_row = as_row(held)
    same = p_row == p_col
    before = last(same & earlier)
    source = jnp.where(before >= 0, look_up(held_row, before), p_col)
    leaves = look_up(held_row, last(same))
    owner = source // rows_dev
    slot = jnp.sum(
        jnp.where((as_row(owner) == owner) & earlier, 1, 0), axis=1, keepdims=True
    )
    code = owner * slots + jnp.minimum(slot, slots - 1)
    mine = (owner == me) & (slot == over)
    offset = source - me * rows_dev
    wide = lax.broadcasted_iota(jnp.int32, (NB, PROWS * slots), 1)
    code_wide = owner * slots + slot
    hit = (code_wide == wide) & (slot < slots)
    table[pl.ds(0, 1), pl.ds(0, NB)] = as_row(code)
    table[pl.ds(1, 1), pl.ds(0, NB)] = jnp.sum(
        jnp.where(mine, offset, 0), axis=0, keepdims=True
    )
    table[pl.ds(2, 1), pl.ds(0, NB)] = (
        jnp.sum(jnp.where(mine & (source >= NB), offset + 1, 0), axis=0, keepdims=True) - 1
    )
    table[pl.ds(3, 1), :] = jnp.sum(jnp.where(hit, leaves, 0), axis=0, keepdims=True)
    table[pl.ds(4, 1), pl.ds(0, NB)] = as_row(slot)


def exchange_kernel(
    slots,
    pivots, matrix,
    resident, gathered, panel, inverse, returned, place, most,
    table, plan, picks, received, ordered, top, top_a, top_b, back, corner,
    row_send, row_recv, ret_send, ret_recv, ring_send, ring_recv,
    top_send, top_recv, panel_send, panel_recv, inv_send, inv_recv, own_sem, load_sem,
):
    half = NB // 2
    rows_dev = matrix.shape[0]
    me = lax.axis_index("prow")
    col = lax.axis_index("pcol")
    x, y = me // SIDE, me % SIDE
    z, core = col // 2, col % 2
    sent = []

    def block(q):
        return pl.ds(pl.multiple_of(q * NB, NB), NB)

    def remote(src, dst, send_sem, recv_sem, device):
        return pltpu.make_async_remote_copy(
            src_ref=src, dst_ref=dst, send_sem=send_sem, recv_sem=recv_sem, device_id=device
        )

    z_up, z_down = ((z + 1) % 4) * 2 + core, ((z + 3) % 4) * 2 + core
    other = z * 2 + 1 - core
    barrier = pltpu.get_barrier_semaphore()
    for d in range(1, PROWS):
        pl.semaphore_signal(barrier, inc=1, device_id={"prow": (me + d) % PROWS})
    for c in (z_up, z_down, other):
        pl.semaphore_signal(barrier, inc=1, device_id={"pcol": c})
    pl.semaphore_wait(barrier, PROWS - 1 + 3)

    def top_x(d):
        return remote(
            matrix.at[pl.ds(0, half), pl.ds(d * SIDE * NB, SIDE * NB)], top_a,
            top_send.at[d], top_recv.at[0], {"prow": d * SIDE},
        )

    def top_y(d, k):
        return remote(
            matrix.at[pl.ds(half, half), pl.ds((k * SIDE + d) * NB, NB)],
            top_b.at[:, pl.ds(k * NB, NB)],
            top_send.at[4 + 4 * d + k], top_recv.at[1 + k], {"prow": d},
        )

    top_own = [
        pltpu.make_async_copy(
            matrix.at[pl.ds(0, half), pl.ds(0, SIDE * NB)], top_a, own_sem.at[1]
        )
    ] + [
        pltpu.make_async_copy(
            matrix.at[pl.ds(half, half), pl.ds(k * SIDE * NB, NB)],
            top_b.at[:, pl.ds(k * NB, NB)], own_sem.at[2 + k],
        )
        for k in range(SIDE)
    ]
    diagonal = pltpu.make_async_copy(matrix.at[pl.ds(0, NB), pl.ds(0, NB)], corner, own_sem.at[6])

    @pl.when(me == 0)
    def _():
        for d in (1, 3, 2):
            top_x(d).start()
            for k in range(SIDE):
                top_y(d, k).start()
        for c in top_own:
            c.start()

    @pl.when((me == 0) & (col == 0))
    def _():
        diagonal.start()

    halves = [pl.ds(0, rows_dev // 2), pl.ds(rows_dev // 2, rows_dev // 2)]
    first_panel = matrix.at[:, pl.ds(0, NB)]

    def panel_first(h, k, to):
        return remote(
            first_panel.at[halves[h]], panel.at[halves[h]],
            panel_send.at[k], panel_recv.at[h], {"pcol": to},
        )

    def panel_next(h, k, to):
        return remote(
            panel.at[halves[h]], panel.at[halves[h]],
            panel_send.at[k], panel_recv.at[h], {"pcol": to},
        )

    panel_own = pltpu.make_async_copy(first_panel, panel, own_sem.at[7])

    @pl.when(col == 0)
    def _():
        panel_first(0, 0, z_up).start()
        panel_first(1, 1, z_down).start()
        panel_first(1, 2, z_up).start()
        panel_first(0, 3, z_down).start()
        panel_first(0, 4, other).start()
        panel_first(1, 5, other).start()
        panel_own.start()

    loads = []
    for k in range(LOADS):
        part = pl.ds(k * (rows_dev // LOADS), rows_dev // LOADS)
        loads.append(
            pltpu.make_async_copy(matrix.at[part, :], resident.at[part, :], load_sem.at[k])
        )
        loads[-1].start()

    swap_plan(slots, pivots, me, rows_dev, table)
    plan_copy = pltpu.make_async_copy(table, plan, own_sem.at[9])
    plan_copy.start()
    place[...] = table[pl.ds(2, 1), pl.ds(0, NB)]
    plan_copy.wait()
    for c in loads:
        c.wait()

    def pick(s, carry):
        picks[pl.ds(s, 1), :] = resident[pl.ds(plan[1, s], 1), :]
        return carry

    lax.fori_loop(0, slots, pick, 0, unroll=4)

    def row_copy(d):
        peer = (me + d) % PROWS
        return remote(
            picks.at[:, block(peer)],
            received.at[pl.ds(pl.multiple_of(me * slots, 8), slots)],
            row_send.at[d], row_recv.at[d], {"prow": peer},
        )

    def row_start(d, carry):
        row_copy(d).start()
        return carry

    def row_wait(d, carry):
        row_copy(d).wait_recv()
        return carry

    def row_sent(d, carry):
        row_copy(d).wait_send()
        return carry

    lax.fori_loop(1, PROWS, row_start, 0)

    def inv_copy(k, device):
        return remote(inverse, inverse, inv_send.at[k], inv_recv.at[0], device)

    @pl.when((me == 0) & (col == 0))
    def _():
        diagonal.wait()
        inverse[...] = invert_unit_lower(corner[...])
        for d in range(1, SIDE):
            inv_copy(d, {"prow": d * SIDE}).start()

    own_rows = pltpu.make_async_copy(
        picks.at[:, block(me)],
        received.at[pl.ds(pl.multiple_of(me * slots, 8), slots)],
        own_sem.at[0],
    )
    own_rows.start()
    own_rows.wait()
    lax.fori_loop(1, PROWS, row_wait, 0)

    def order(j, carry):
        ordered[pl.ds(j, 1), :] = received[pl.ds(plan[0, j], 1), :]
        return carry

    lax.fori_loop(0, NB, order, 0, unroll=8)
    gathered[:, block(me)] = ordered[...]

    def spot(o, along, across):
        dx, dy = (along, across) if o == 0 else (across, along)
        return ((x + dx + SIDE) % SIDE) * SIDE + (y + dy + SIDE) % SIDE

    def ring_copy(o, q, sem, device):
        ref = gathered.at[pl.ds(o * half, half), block(q)]
        return remote(ref, ref, ring_send.at[o, sem], ring_recv.at[o, sem], {"prow": device})

    def ring_start(o, q, sem, device):
        c = ring_copy(o, q, sem, device)
        c.start()
        sent.append(c)

    for d in (2, 1, 3):
        for o in (0, 1):
            ring_start(o, me, d, spot(o, d, 0))
    for d in (2, 1, 3):
        for o in (0, 1):
            ring_start(o, me, 3 + d, spot(o, 0, d))

    def top_leg(a, d):
        if a == 0:
            src, dst, device = top_a, top.at[pl.ds(0, half)], x * SIDE + d
        else:
            src, dst, device = top_b, top.at[pl.ds(half, half)], d * SIDE + y
        return remote(
            src.at[:, pl.ds(d * NB, NB)], dst,
            top_send.at[20 + 4 * a + d], top_recv.at[5 + a], {"prow": device},
        )

    @pl.when(me == 0)
    def _():
        for c in top_own:
            c.wait()

    @pl.when(y == 0)
    def _():
        @pl.when(x != 0)
        def _():
            top_x(1).wait_recv()

        for d in range(1, SIDE):
            top_leg(0, d).start()
        top[pl.ds(0, half), :] = top_a[:, pl.ds(0, NB)]

    @pl.when(x == 0)
    def _():
        @pl.when(y != 0)
        def _():
            for k in range(SIDE):
                top_y(1, k).wait_recv()

        for d in range(1, SIDE):
            top_leg(1, d).start()
        top[pl.ds(half, half), :] = top_b[:, pl.ds(0, NB)]

    for e in (1, 3, 2):
        for o in (0, 1):
            q = spot(o, -e, 0)
            ring_copy(o, q, e, me).wait_recv()
            for d in (2, 1, 3):
                ring_start(o, q, 3 + 3 * e + d, spot(o, 0, d))

    @pl.when((col == 0) & (y == 0))
    def _():
        @pl.when(x != 0)
        def _():
            inv_copy(0, {"pcol": other}).wait_recv()

        for d in range(1, SIDE):
            inv_copy(3 + d, {"prow": x * SIDE + d}).start()

    def panel_leg(h):
        @pl.when((core == 0) & (z > 0))
        def _():
            panel_next(h, 0, other).wait_recv()
            panel_next(h, 4 + h, other).start()

            @pl.when((z == 1) if h == 0 else (z == 3))
            def _():
                panel_next(h, 0, 4).start()

    panel_leg(0)
    panel_leg(1)

    @pl.when(y != 0)
    def _():
        top_leg(0, 1).wait_recv()

    @pl.when(x != 0)
    def _():
        top_leg(1, 1).wait_recv()

    def back_rows(r, carry):
        for s in range(slots):
            index = plan[3, r * slots + s]
            back[pl.ds(r * slots + s, 1), :] = top[pl.ds(index, 1), :]
        return carry

    lax.fori_loop(0, PROWS, back_rows, 0)

    def ret_copy(d):
        peer = (me + d) % PROWS
        return remote(
            back.at[pl.ds(pl.multiple_of(peer * slots, 8), slots)],
            returned.at[:, block(me)],
            ret_send.at[d], ret_recv.at[d], {"prow": peer},
        )

    def ret_start(d, carry):
        ret_copy(d).start()
        return carry

    def ret_wait(d, carry):
        peer = (me - d + PROWS) % PROWS
        remote(
            back.at[pl.ds(0, slots)], returned.at[:, block(peer)],
            ret_send.at[d], ret_recv.at[d], {"prow": peer},
        ).wait_recv()
        return carry

    def ret_sent(d, carry):
        ret_copy(d).wait_send()
        return carry

    lax.fori_loop(1, PROWS, ret_start, 0)
    ret_own = pltpu.make_async_copy(
        back.at[pl.ds(pl.multiple_of(me * slots, 8), slots)],
        returned.at[:, block(me)], own_sem.at[8],
    )
    ret_own.start()

    @pl.when(col == 0)
    def _():
        @pl.when(y != 0)
        def _():
            inv_copy(0, {"pcol": other}).wait_recv()

        inv_copy(7, {"pcol": z_up}).start()
        inv_copy(8, {"pcol": z_down}).start()
        inv_copy(9, {"pcol": other}).start()

    for e in (0, 1, 3, 2):
        for d in (1, 3, 2):
            for o in (0, 1):
                ring_copy(o, spot(o, -e, -d), 3 + 3 * e + d, me).wait_recv()

    @pl.when(col != 0)
    def _():
        inv_copy(0, {"pcol": other}).wait_recv()

        @pl.when(core == 0)
        def _():
            inv_copy(9, {"pcol": other}).start()

            @pl.when(z == 1)
            def _():
                inv_copy(7, {"pcol": 4}).start()

    most[0] = lax.fori_loop(0, NB, lambda j, m: jnp.maximum(m, plan[4, j]), 0, unroll=8)
    lax.fori_loop(1, PROWS, ret_wait, 0)
    ret_own.wait()

    @pl.when(core == 1)
    def _():
        panel_next(0, 0, other).wait_recv()
        panel_next(1, 0, other).wait_recv()

    for c in sent:
        c.wait_send()
    lax.fori_loop(1, PROWS, row_sent, 0)
    lax.fori_loop(1, PROWS, ret_sent, 0)

    @pl.when(me == 0)
    def _():
        for d in (1, 3, 2):
            top_x(d).wait_send()
            for k in range(SIDE):
                top_y(d, k).wait_send()

    @pl.when(y == 0)
    def _():
        for d in range(1, SIDE):
            top_leg(0, d).wait_send()

    @pl.when(x == 0)
    def _():
        for d in range(1, SIDE):
            top_leg(1, d).wait_send()

    @pl.when(col == 0)
    def _():
        panel_own.wait()
        for h, k in ((0, 0), (1, 1), (1, 2), (0, 3), (0, 4), (1, 5)):
            panel_first(h, k, other).wait_send()

        @pl.when(me == 0)
        def _():
            for d in range(1, SIDE):
                inv_copy(d, {"prow": d * SIDE}).wait_send()

        @pl.when(y == 0)
        def _():
            for d in range(1, SIDE):
                inv_copy(3 + d, {"prow": x * SIDE + d}).wait_send()

        for k in (7, 8, 9):
            inv_copy(k, {"pcol": other}).wait_send()

    @pl.when((core == 0) & (z > 0))
    def _():
        panel_next(0, 4, other).wait_send()
        panel_next(1, 5, other).wait_send()
        inv_copy(9, {"pcol": other}).wait_send()

        @pl.when(z == 1)
        def _():
            panel_next(0, 0, other).wait_send()
            inv_copy(7, {"pcol": other}).wait_send()

        @pl.when(z == 3)
        def _():
            panel_next(1, 0, other).wait_send()


def exchange(slots, collective_id, matrix, pivots):
    rows_dev, cols_dev = matrix.shape
    f32, i32 = jnp.float32, jnp.int32
    smem = pl.BlockSpec(memory_space=pltpu.SMEM)
    vmem = pl.BlockSpec(memory_space=pltpu.VMEM)
    hbm = pl.BlockSpec(memory_space=pltpu.HBM)
    dma = pltpu.SemaphoreType.DMA
    return pl.pallas_call(
        functools.partial(exchange_kernel, slots),
        out_shape=[
            pltpu.VMEM((rows_dev, cols_dev), f32),
            jax.ShapeDtypeStruct((NB, cols_dev), f32),
            jax.ShapeDtypeStruct((rows_dev, NB), f32),
            jax.ShapeDtypeStruct((NB, NB), f32),
            jax.ShapeDtypeStruct((slots, cols_dev), f32),
            jax.ShapeDtypeStruct((1, NB), i32),
            jax.ShapeDtypeStruct((1,), i32),
        ],
        in_specs=[vmem, hbm],
        out_specs=[vmem, vmem, vmem, vmem, vmem, vmem, smem],
        scratch_shapes=[
            pltpu.VMEM((8, PROWS * slots), i32),
            pltpu.SMEM((8, PROWS * slots), i32),
            pltpu.VMEM((slots, cols_dev), f32),
            pltpu.VMEM((PROWS * slots, NB), f32),
            pltpu.VMEM((NB, NB), f32),
            pltpu.VMEM((NB, NB), f32),
            pltpu.VMEM((NB // 2, SIDE * NB), f32),
            pltpu.VMEM((NB // 2, SIDE * NB), f32),
            pltpu.VMEM((PROWS * slots, NB), f32),
            pltpu.VMEM((NB, NB), f32),
            dma((PROWS,)), dma((PROWS,)), dma((PROWS,)), dma((PROWS,)),
            dma((2, 16)), dma((2, 16)),
            dma((28,)), dma((7,)), dma((6,)), dma((2,)), dma((10,)), dma((1,)), dma((10,)),
            dma((LOADS,)),
        ],
        compiler_params=pltpu.CompilerParams(
            collective_id=collective_id, has_side_effects=True, vmem_limit_bytes=24 * MIB
        ),
        name="exchange_%d" % slots,
    )(pivots, pltpu.with_memory_space_constraint(matrix, pltpu.HBM))


def split(value):
    high = value.astype(jnp.bfloat16)
    return high, (value - high.astype(jnp.float32)).astype(jnp.bfloat16)


def stacked(value):
    high, low = split(value)
    return jnp.concatenate([high, low, high], axis=1)


def update_kernel(
    slots, place, matrix, gathered, panel, inverse, returned, out,
    result, factor, chosen, chosen_factor, fixed, sems,
):
    me = lax.axis_index("prow")
    col = lax.axis_index("pcol")
    factor[...] = stacked(panel[...])

    def choose(s, carry):
        p = jnp.maximum(place[0, s], 0)
        chosen[pl.ds(s, 1), :] = panel[pl.ds(p, 1), :]
        return carry

    lax.fori_loop(0, slots, choose, 0, unroll=4)
    chosen_factor[...] = stacked(chosen[...])

    def write(n):
        return pltpu.make_async_copy(
            result.at[:, pl.ds(n * WIDE, WIDE)], out.at[:, pl.ds(n * WIDE, WIDE)], sems.at[n]
        )

    parts = matrix.shape[1] // WIDE
    for n in range(parts):
        here = pl.ds(n * WIDE, WIDE)
        upper = jnp.dot(
            inverse[...], gathered[:, here], precision=HIGHEST, preferred_element_type=jnp.float32
        )
        high, low = split(upper)
        terms = jnp.concatenate([high, high, low], axis=0)
        result[:, here] = matrix[:, here] - jnp.dot(
            factor[...], terms, preferred_element_type=jnp.float32
        )
        fixed[...] = returned[:, here] - jnp.dot(
            chosen_factor[...], terms, preferred_element_type=jnp.float32
        )

        def fix(s, carry):
            @pl.when(place[0, s] >= 0)
            def _():
                result[pl.ds(place[0, s], 1), here] = fixed[pl.ds(s, 1), :]

            return carry

        lax.fori_loop(0, slots, fix, 0)

        @pl.when(me == 0)
        def _():
            result[pl.ds(0, NB), here] = upper

        if n == 0:

            @pl.when(col == 0)
            def _():
                result[:, pl.ds(0, NB)] = matrix[:, pl.ds(0, NB)]

        write(n).start()
    for n in range(parts):
        write(n).wait()


def update(slots, matrix, gathered, panel, inverse, returned, place):
    rows_dev, cols_dev = matrix.shape
    smem = pl.BlockSpec(memory_space=pltpu.SMEM)
    vmem = pl.BlockSpec(memory_space=pltpu.VMEM)
    return pl.pallas_call(
        functools.partial(update_kernel, slots),
        out_shape=pltpu.HBM(matrix.shape, jnp.float32),
        in_specs=[smem, vmem, vmem, vmem, vmem, vmem],
        out_specs=pl.BlockSpec(memory_space=pltpu.HBM),
        scratch_shapes=[
            pltpu.VMEM((rows_dev, cols_dev), jnp.float32),
            pltpu.VMEM((rows_dev, 3 * NB), jnp.bfloat16),
            pltpu.VMEM((slots, NB), jnp.float32),
            pltpu.VMEM((slots, 3 * NB), jnp.bfloat16),
            pltpu.VMEM((slots, WIDE), jnp.float32),
            pltpu.SemaphoreType.DMA((cols_dev // WIDE,)),
        ],
        compiler_params=pltpu.CompilerParams(vmem_limit_bytes=28 * MIB),
        name="update_%d" % slots,
    )(place, matrix, gathered, panel, inverse, returned)


def local(matrix, pivots):
    pivots = pivots.reshape(1, NB)
    *found, most = exchange(FEW, 0, matrix, pivots)

    def many():
        *found, _ = exchange(NB, 1, matrix, pivots)
        return update(NB, *found)

    return lax.cond(most[0] < FEW, lambda: update(FEW, *found), many)


def solution(mesh):
    placed = (P("prow", "pcol"), P())
    return jax.shard_map(
        local, mesh=mesh, in_specs=placed, out_specs=P("prow", "pcol"), check_vma=False
    )
```

```python
import functools

import jax
import jax.numpy as jnp
from jax import lax
from jax.experimental import pallas as pl
from jax.experimental.pallas import tpu as pltpu
from jax.sharding import PartitionSpec as P

NB = 128
PROWS = 16
SIDE = 4
FEW = 24
MIB = 1024 * 1024
LOADS = 8
WIDE = 256
HIGHEST = lax.Precision.HIGHEST


def invert_unit_lower(block):
    rows = lax.broadcasted_iota(jnp.int32, (NB, NB), 0)
    cols = lax.broadcasted_iota(jnp.int32, (NB, NB), 1)
    eye = jnp.where(rows == cols, 1.0, 0.0).astype(jnp.float32)
    dot = functools.partial(jnp.dot, precision=HIGHEST, preferred_element_type=jnp.float32)
    inverse = eye
    size = 1
    while size < NB:
        corner = (rows // size == cols // size + 1) & (rows // (2 * size) == cols // (2 * size))
        part = jnp.where(corner, block, 0.0)
        if size == 1:
            inverse = eye - part
        else:
            inverse = inverse - dot(dot(inverse, part), inverse)
        size *= 2
    return inverse


def swap_plan(slots, pivots, me, rows_dev, table, note, most):
    shape = (NB, NB)
    down = lax.broadcasted_iota(jnp.int32, shape, 0)
    over = lax.broadcasted_iota(jnp.int32, shape, 1)
    earlier = over < down

    def as_row(column):
        return jnp.sum(jnp.where(down == over, column, 0), axis=0, keepdims=True)

    def as_column(row):
        return jnp.sum(jnp.where(down == over, row, 0), axis=1, keepdims=True)

    def look_up(row, index):
        return jnp.sum(jnp.where(over == index, row, 0), axis=1, keepdims=True)

    def last(where):
        return jnp.max(jnp.where(where, over, -1), axis=1, keepdims=True)

    p_row = pivots[...]
    p_col = as_column(p_row)
    steps = lax.broadcasted_iota(jnp.int32, (NB, 1), 0)
    touched = last((p_row == down) & earlier)
    held = jnp.where(touched >= 0, touched, steps)
    for _ in range(7):
        held = look_up(as_row(held), held)
    held_row = as_row(held)
    same = p_row == p_col
    before = last(same & earlier)
    source = jnp.where(before >= 0, look_up(held_row, before), p_col)
    leaves = look_up(held_row, last(same))
    owner = source // rows_dev
    slot = jnp.sum(
        jnp.where((as_row(owner) == owner) & earlier, 1, 0), axis=1, keepdims=True
    )
    code = owner * slots + jnp.minimum(slot, slots - 1)
    mine = (owner == me) & (slot == over)
    offset = source - me * rows_dev
    wide = lax.broadcasted_iota(jnp.int32, (NB, PROWS * slots), 1)
    code_wide = owner * slots + slot
    hit = (code_wide == wide) & (slot < slots)
    table[pl.ds(0, 1), pl.ds(0, NB)] = as_row(code)
    table[pl.ds(1, 1), pl.ds(0, NB)] = jnp.sum(
        jnp.where(mine, offset, 0), axis=0, keepdims=True
    )
    table[pl.ds(3, 1), :] = jnp.sum(jnp.where(hit, leaves, 0), axis=0, keepdims=True)
    note[pl.ds(0, 1), :] = table[pl.ds(1, 1), pl.ds(0, NB)]
    note[pl.ds(1, 1), :] = jnp.broadcast_to(
        jnp.sum(jnp.where(owner == me, 1, 0), axis=0, keepdims=True), (1, NB)
    )
    most[...] = jnp.broadcast_to(jnp.max(as_row(slot), axis=1, keepdims=True), (1, NB))


def exchange_kernel(
    slots,
    pivots_hbm, matrix,
    resident, gathered, panel, inverse, returned, note, most,
    pivots, table, plan, picks, received, ordered, top, top_a, top_b, back, corner,
    row_send, row_recv, ret_send, ret_recv, ring_send, ring_recv,
    top_send, top_recv, panel_send, panel_recv, inv_send, inv_recv, own_sem, load_sem,
):
    half = NB // 2
    rows_dev = matrix.shape[0]
    me = lax.axis_index("prow")
    col = lax.axis_index("pcol")
    x, y = me // SIDE, me % SIDE
    z, core = col // 2, col % 2
    sent = []

    def block(q):
        return pl.ds(pl.multiple_of(q * NB, NB), NB)

    def remote(src, dst, send_sem, recv_sem, device):
        return pltpu.make_async_remote_copy(
            src_ref=src, dst_ref=dst, send_sem=send_sem, recv_sem=recv_sem, device_id=device
        )

    def ahead(d):
        return jnp.where(me + d >= PROWS, me + d - PROWS, me + d)

    def behind(d):
        return jnp.where(me >= d, me - d, me - d + PROWS)

    z_up = jnp.where(col >= 6, col - 6, col + 2)
    z_down = jnp.where(col >= 2, col - 2, col + 6)
    other = jnp.where(core == 0, col + 1, col - 1)
    pivots_in = pltpu.make_async_copy(pivots_hbm, pivots, own_sem.at[10])
    pivots_in.start()
    loads = []
    for k in range(LOADS):
        part = pl.ds(k * (rows_dev // LOADS), rows_dev // LOADS)
        loads.append(
            pltpu.make_async_copy(matrix.at[part, :], resident.at[part, :], load_sem.at[k])
        )
        loads[-1].start()
    barrier = pltpu.get_barrier_semaphore()
    for d in range(1, PROWS):
        pl.semaphore_signal(barrier, inc=1, device_id={"prow": ahead(d)})
    for c in (z_up, z_down, other):
        pl.semaphore_signal(barrier, inc=1, device_id={"pcol": c})
    pl.semaphore_wait(barrier, PROWS - 1 + 3)

    def top_x(d):
        return remote(
            matrix.at[pl.ds(0, half), pl.ds(d * SIDE * NB, SIDE * NB)], top_a,
            top_send.at[d], top_recv.at[0], {"prow": d * SIDE},
        )

    def top_y(d, k):
        return remote(
            matrix.at[pl.ds(half, half), pl.ds((k * SIDE + d) * NB, NB)],
            top_b.at[:, pl.ds(k * NB, NB)],
            top_send.at[4 + 4 * d + k], top_recv.at[1 + k], {"prow": d},
        )

    top_own = [
        pltpu.make_async_copy(
            matrix.at[pl.ds(0, half), pl.ds(0, SIDE * NB)], top_a, own_sem.at[1]
        )
    ] + [
        pltpu.make_async_copy(
            matrix.at[pl.ds(half, half), pl.ds(k * SIDE * NB, NB)],
            top_b.at[:, pl.ds(k * NB, NB)], own_sem.at[2 + k],
        )
        for k in range(SIDE)
    ]
    diagonal = pltpu.make_async_copy(matrix.at[pl.ds(0, NB), pl.ds(0, NB)], corner, own_sem.at[6])

    @pl.when(me == 0)
    def _():
        for d in (1, 3, 2):
            top_x(d).start()
            for k in range(SIDE):
                top_y(d, k).start()
        for c in top_own:
            c.start()

    @pl.when((me == 0) & (col == 0))
    def _():
        diagonal.start()

    halves = [pl.ds(0, rows_dev // 2), pl.ds(rows_dev // 2, rows_dev // 2)]
    first_panel = matrix.at[:, pl.ds(0, NB)]

    def panel_first(h, k, to):
        return remote(
            first_panel.at[halves[h]], panel.at[halves[h]],
            panel_send.at[k], panel_recv.at[h], {"pcol": to},
        )

    def panel_next(h, k, to):
        return remote(
            panel.at[halves[h]], panel.at[halves[h]],
            panel_send.at[k], panel_recv.at[h], {"pcol": to},
        )

    panel_own = pltpu.make_async_copy(first_panel, panel, own_sem.at[7])

    @pl.when(col == 0)
    def _():
        panel_first(0, 0, z_up).start()
        panel_first(1, 1, z_down).start()
        panel_first(1, 2, z_up).start()
        panel_first(0, 3, z_down).start()
        panel_first(0, 4, other).start()
        panel_first(1, 5, other).start()
        panel_own.start()

    pivots_in.wait()
    swap_plan(slots, pivots, me, rows_dev, table, note, most)
    plan_copy = pltpu.make_async_copy(table, plan, own_sem.at[9])
    plan_copy.start()
    plan_copy.wait()
    for c in loads:
        c.wait()

    def pick(s, carry):
        picks[pl.ds(s, 1), :] = resident[pl.ds(plan[1, s], 1), :]
        return carry

    lax.fori_loop(0, slots, pick, 0, unroll=4)

    def row_copy(d):
        peer = ahead(d)
        return remote(
            picks.at[:, block(peer)],
            received.at[pl.ds(pl.multiple_of(me * slots, 8), slots)],
            row_send.at[d], row_recv.at[d], {"prow": peer},
        )

    def row_start(d, carry):
        row_copy(d).start()
        return carry

    def row_wait(d, carry):
        row_copy(d).wait_recv()
        return carry

    def row_sent(d, carry):
        row_copy(d).wait_send()
        return carry

    for d in (10, 2, 8, 6, 9, 7, 11, 5, 13, 3, 14, 1, 15, 4, 12):
        row_start(d, 0)

    def inv_copy(k, device):
        return remote(inverse, inverse, inv_send.at[k], inv_recv.at[0], device)

    @pl.when((me == 0) & (col == 0))
    def _():
        diagonal.wait()
        inverse[...] = invert_unit_lower(corner[...])
        for d in range(1, SIDE):
            inv_copy(d, {"prow": d * SIDE}).start()

    own_rows = pltpu.make_async_copy(
        picks.at[:, block(me)],
        received.at[pl.ds(pl.multiple_of(me * slots, 8), slots)],
        own_sem.at[0],
    )
    own_rows.start()
    def top_leg(a, d):
        if a == 0:
            src, dst, device = top_a, top.at[pl.ds(0, half)], x * SIDE + d
        else:
            src, dst, device = top_b, top.at[pl.ds(half, half)], d * SIDE + y
        return remote(
            src.at[:, pl.ds(d * NB, NB)], dst,
            top_send.at[20 + 4 * a + d], top_recv.at[5 + a], {"prow": device},
        )

    @pl.when(me == 0)
    def _():
        for c in top_own:
            c.wait()

    @pl.when(y == 0)
    def _():
        @pl.when(x != 0)
        def _():
            top_x(1).wait_recv()

        for d in range(1, SIDE):
            top_leg(0, d).start()
        top[pl.ds(0, half), :] = top_a[:, pl.ds(0, NB)]

    @pl.when(x == 0)
    def _():
        @pl.when(y != 0)
        def _():
            for k in range(SIDE):
                top_y(1, k).wait_recv()

        for d in range(1, SIDE):
            top_leg(1, d).start()
        top[pl.ds(half, half), :] = top_b[:, pl.ds(0, NB)]

    def panel_leg(h, there):
        @pl.when((core == 0) & there)
        def _():
            panel_next(h, 0, other).wait_recv()
            panel_next(h, 4 + h, other).start()

            @pl.when((z == 1) if h == 0 else (z == 3))
            def _():
                panel_next(h, 0, 4).start()

    for h in (0, 1):
        panel_leg(h, z == 1 if h == 0 else z == 3)
    for h in (0, 1):
        panel_leg(h, z == 3 if h == 0 else z == 1)

    own_rows.wait()
    lax.fori_loop(1, PROWS, row_wait, 0)

    def order(j, carry):
        ordered[pl.ds(j, 1), :] = received[pl.ds(plan[0, j], 1), :]
        return carry

    lax.fori_loop(0, NB, order, 0, unroll=8)
    gathered[:, block(me)] = ordered[...]

    def spot(o, along, across):
        dx, dy = (along, across) if o == 0 else (across, along)
        xx, yy = x + dx, y + dy
        if dx:
            xx = jnp.where(xx >= SIDE, xx - SIDE, jnp.where(xx < 0, xx + SIDE, xx))
        if dy:
            yy = jnp.where(yy >= SIDE, yy - SIDE, jnp.where(yy < 0, yy + SIDE, yy))
        return xx * SIDE + yy

    def ring_copy(o, q, sem, device):
        ref = gathered.at[pl.ds(o * half, half), block(q)]
        return remote(ref, ref, ring_send.at[o, sem], ring_recv.at[o, sem], {"prow": device})

    def ring_start(o, q, sem, device):
        c = ring_copy(o, q, sem, device)
        c.start()
        sent.append(c)

    for d in (2, 1, 3):
        for o in (0, 1):
            ring_start(o, me, d, spot(o, d, 0))
    for d in (2, 1, 3):
        for o in (0, 1):
            ring_start(o, me, 3 + d, spot(o, 0, d))

    for e in (1, 3, 2):
        for o in (0, 1):
            q = spot(o, -e, 0)
            ring_copy(o, q, e, me).wait_recv()
            for d in (2, 1, 3):
                ring_start(o, q, 3 + 3 * e + d, spot(o, 0, d))

    @pl.when((col == 0) & (y == 0))
    def _():
        @pl.when(x != 0)
        def _():
            inv_copy(0, {"pcol": other}).wait_recv()

        for d in range(1, SIDE):
            inv_copy(3 + d, {"prow": x * SIDE + d}).start()

    panel_leg(0, z == 2)
    panel_leg(1, z == 2)

    @pl.when(y != 0)
    def _():
        top_leg(0, 1).wait_recv()

    @pl.when(x != 0)
    def _():
        top_leg(1, 1).wait_recv()

    def back_rows(r, carry):
        for s in range(slots):
            index = plan[3, r * slots + s]
            back[pl.ds(r * slots + s, 1), :] = top[pl.ds(index, 1), :]
        return carry

    lax.fori_loop(0, PROWS, back_rows, 0)

    def ret_copy(d):
        peer = ahead(d)
        return remote(
            back.at[pl.ds(pl.multiple_of(peer * slots, 8), slots)],
            returned.at[:, block(me)],
            ret_send.at[d], ret_recv.at[d], {"prow": peer},
        )

    def ret_start(d, carry):
        ret_copy(d).start()
        return carry

    def ret_wait(d, carry):
        peer = behind(d)
        remote(
            back.at[pl.ds(0, slots)], returned.at[:, block(peer)],
            ret_send.at[d], ret_recv.at[d], {"prow": peer},
        ).wait_recv()
        return carry

    def ret_sent(d, carry):
        ret_copy(d).wait_send()
        return carry

    lax.fori_loop(1, PROWS, ret_start, 0)
    ret_own = pltpu.make_async_copy(
        back.at[pl.ds(pl.multiple_of(me * slots, 8), slots)],
        returned.at[:, block(me)], own_sem.at[8],
    )
    ret_own.start()

    @pl.when(col == 0)
    def _():
        @pl.when(y != 0)
        def _():
            inv_copy(0, {"pcol": other}).wait_recv()

        inv_copy(7, {"pcol": z_up}).start()
        inv_copy(8, {"pcol": z_down}).start()
        inv_copy(9, {"pcol": other}).start()

    for e in (0, 1, 3, 2):
        for d in (1, 3, 2):
            for o in (0, 1):
                ring_copy(o, spot(o, -e, -d), 3 + 3 * e + d, me).wait_recv()

    @pl.when(col != 0)
    def _():
        inv_copy(0, {"pcol": other}).wait_recv()

        @pl.when(core == 0)
        def _():
            inv_copy(9, {"pcol": other}).start()

            @pl.when(z == 1)
            def _():
                inv_copy(7, {"pcol": 4}).start()

    lax.fori_loop(1, PROWS, ret_wait, 0)
    ret_own.wait()

    @pl.when(core == 1)
    def _():
        panel_next(0, 0, other).wait_recv()
        panel_next(1, 0, other).wait_recv()

    for c in sent:
        c.wait_send()
    lax.fori_loop(1, PROWS, row_sent, 0)
    lax.fori_loop(1, PROWS, ret_sent, 0)

    @pl.when(me == 0)
    def _():
        for d in (1, 3, 2):
            top_x(d).wait_send()
            for k in range(SIDE):
                top_y(d, k).wait_send()

    @pl.when(y == 0)
    def _():
        for d in range(1, SIDE):
            top_leg(0, d).wait_send()

    @pl.when(x == 0)
    def _():
        for d in range(1, SIDE):
            top_leg(1, d).wait_send()

    @pl.when(col == 0)
    def _():
        panel_own.wait()
        for h, k in ((0, 0), (1, 1), (1, 2), (0, 3), (0, 4), (1, 5)):
            panel_first(h, k, other).wait_send()

        @pl.when(me == 0)
        def _():
            for d in range(1, SIDE):
                inv_copy(d, {"prow": d * SIDE}).wait_send()

        @pl.when(y == 0)
        def _():
            for d in range(1, SIDE):
                inv_copy(3 + d, {"prow": x * SIDE + d}).wait_send()

        for k in (7, 8, 9):
            inv_copy(k, {"pcol": other}).wait_send()

    @pl.when((core == 0) & (z > 0))
    def _():
        panel_next(0, 4, other).wait_send()
        panel_next(1, 5, other).wait_send()
        inv_copy(9, {"pcol": other}).wait_send()

        @pl.when(z == 1)
        def _():
            panel_next(0, 0, other).wait_send()
            inv_copy(7, {"pcol": other}).wait_send()

        @pl.when(z == 3)
        def _():
            panel_next(1, 0, other).wait_send()


def exchange(slots, collective_id, matrix, pivots):
    rows_dev, cols_dev = matrix.shape
    f32, i32 = jnp.float32, jnp.int32
    vmem = pl.BlockSpec(memory_space=pltpu.VMEM)
    hbm = pl.BlockSpec(memory_space=pltpu.HBM)
    dma = pltpu.SemaphoreType.DMA
    return pl.pallas_call(
        functools.partial(exchange_kernel, slots),
        out_shape=[
            pltpu.VMEM((rows_dev, cols_dev), f32),
            jax.ShapeDtypeStruct((NB, cols_dev), f32),
            jax.ShapeDtypeStruct((rows_dev, NB), f32),
            jax.ShapeDtypeStruct((NB, NB), f32),
            jax.ShapeDtypeStruct((slots, cols_dev), f32),
            jax.ShapeDtypeStruct((2, NB), i32),
            jax.ShapeDtypeStruct((1, NB), i32),
        ],
        in_specs=[hbm, hbm],
        out_specs=[vmem] * 7,
        scratch_shapes=[
            pltpu.VMEM((1, NB), i32),
            pltpu.VMEM((8, PROWS * slots), i32),
            pltpu.SMEM((8, PROWS * slots), i32),
            pltpu.VMEM((slots, cols_dev), f32),
            pltpu.VMEM((PROWS * slots, NB), f32),
            pltpu.VMEM((NB, NB), f32),
            pltpu.VMEM((NB, NB), f32),
            pltpu.VMEM((NB // 2, SIDE * NB), f32),
            pltpu.VMEM((NB // 2, SIDE * NB), f32),
            pltpu.VMEM((PROWS * slots, NB), f32),
            pltpu.VMEM((NB, NB), f32),
            dma((PROWS,)), dma((PROWS,)), dma((PROWS,)), dma((PROWS,)),
            dma((2, 16)), dma((2, 16)),
            dma((28,)), dma((7,)), dma((6,)), dma((2,)), dma((10,)), dma((1,)), dma((11,)),
            dma((LOADS,)),
        ],
        compiler_params=pltpu.CompilerParams(
            collective_id=collective_id, has_side_effects=True, vmem_limit_bytes=24 * MIB
        ),
        name="exchange_%d" % slots,
    )(pivots, pltpu.with_memory_space_constraint(matrix, pltpu.HBM))


def split(value):
    high = value.astype(jnp.bfloat16)
    return high, (value - high.astype(jnp.float32)).astype(jnp.bfloat16)


def stacked(value):
    high, low = split(value)
    return jnp.concatenate([high, low, high], axis=1)


def update_kernel(
    note, block, gathered, panel, inverse, returned, out, matrix,
    notes, result, factor, note_sem, sems,
):
    me = lax.axis_index("prow")
    col = lax.axis_index("pcol")
    note_copy = pltpu.make_async_copy(note, notes, note_sem.at[0])
    note_copy.start()
    factor[...] = stacked(panel[...])
    solve = stacked(inverse[...])
    note_copy.wait()

    def replace(s, carry):
        matrix[pl.ds(notes[0, s], 1), :] = returned[pl.ds(s, 1), :]
        return carry

    lax.fori_loop(0, notes[1, 0], replace, 0)

    def write(n):
        return pltpu.make_async_copy(
            result.at[:, pl.ds(n * WIDE, WIDE)], out.at[:, pl.ds(n * WIDE, WIDE)], sems.at[n]
        )

    def terms(value):
        high, low = split(value)
        return jnp.concatenate([high, high, low], axis=0)

    parts = matrix.shape[1] // WIDE
    for n in range(parts):
        here = pl.ds(n * WIDE, WIDE)
        upper = jnp.dot(solve, terms(gathered[:, here]), preferred_element_type=jnp.float32)
        result[:, here] = matrix[:, here] - jnp.dot(
            factor[...], terms(upper), preferred_element_type=jnp.float32
        )

        @pl.when(me == 0)
        def _():
            result[pl.ds(0, NB), here] = upper

        if n == 0:

            @pl.when(col == 0)
            def _():
                result[:, pl.ds(0, NB)] = panel[...]

        write(n).start()
    for n in range(parts):
        write(n).wait()


def update(matrix, gathered, panel, inverse, returned, note):
    rows_dev, cols_dev = matrix.shape
    vmem = pl.BlockSpec(memory_space=pltpu.VMEM)
    out, _ = pl.pallas_call(
        update_kernel,
        out_shape=[
            pltpu.HBM(matrix.shape, jnp.float32), pltpu.VMEM(matrix.shape, jnp.float32)
        ],
        in_specs=[vmem] * 6,
        out_specs=[pl.BlockSpec(memory_space=pltpu.HBM), vmem],
        input_output_aliases={1: 1},
        scratch_shapes=[
            pltpu.SMEM((2, NB), jnp.int32),
            pltpu.VMEM((rows_dev, cols_dev), jnp.float32),
            pltpu.VMEM((rows_dev, 3 * NB), jnp.bfloat16),
            pltpu.SemaphoreType.DMA((1,)),
            pltpu.SemaphoreType.DMA((cols_dev // WIDE,)),
        ],
        compiler_params=pltpu.CompilerParams(vmem_limit_bytes=28 * MIB),
        name="update",
    )(note, matrix, gathered, panel, inverse, returned)
    return out


def local(matrix, pivots):
    pivots = pivots.reshape(1, NB)
    *found, most = exchange(FEW, 0, matrix, pivots)

    def many():
        *found, _ = exchange(NB, 1, matrix, pivots)
        return update(*found)

    return lax.cond(most[0, 0] < FEW, lambda: update(*found), many)


def solution(mesh):
    placed = (P("prow", "pcol"), P())
    return jax.shard_map(
        local, mesh=mesh, in_specs=placed, out_specs=P("prow", "pcol"), check_vma=False
    )
```

```python
import functools

import jax
import jax.numpy as jnp
from jax import lax
from jax.experimental import pallas as pl
from jax.experimental.pallas import tpu as pltpu
from jax.sharding import PartitionSpec as P

NB = 128
PROWS = 16
SIDE = 4
FEW = 24
MIB = 1024 * 1024
LOADS = 8
WIDE = 256
HIGHEST = lax.Precision.HIGHEST


def invert_unit_lower(block):
    rows = lax.broadcasted_iota(jnp.int32, (NB, NB), 0)
    cols = lax.broadcasted_iota(jnp.int32, (NB, NB), 1)
    eye = jnp.where(rows == cols, 1.0, 0.0).astype(jnp.float32)
    dot = functools.partial(jnp.dot, precision=HIGHEST, preferred_element_type=jnp.float32)
    inverse = eye
    size = 1
    while size < NB:
        corner = (rows // size == cols // size + 1) & (rows // (2 * size) == cols // (2 * size))
        part = jnp.where(corner, block, 0.0)
        if size == 1:
            inverse = eye - part
        else:
            inverse = inverse - dot(dot(inverse, part), inverse)
        size *= 2
    return inverse


def swap_plan(slots, pivots, me, rows_dev, table, note, most):
    shape = (NB, NB)
    down = lax.broadcasted_iota(jnp.int32, shape, 0)
    over = lax.broadcasted_iota(jnp.int32, shape, 1)
    earlier = over < down

    def as_row(column):
        return jnp.sum(jnp.where(down == over, column, 0), axis=0, keepdims=True)

    def as_column(row):
        return jnp.sum(jnp.where(down == over, row, 0), axis=1, keepdims=True)

    def look_up(row, index):
        return jnp.sum(jnp.where(over == index, row, 0), axis=1, keepdims=True)

    def last(where):
        return jnp.max(jnp.where(where, over, -1), axis=1, keepdims=True)

    p_row = pivots[...]
    p_col = as_column(p_row)
    steps = lax.broadcasted_iota(jnp.int32, (NB, 1), 0)
    touched = last((p_row == down) & earlier)
    held = jnp.where(touched >= 0, touched, steps)
    for _ in range(7):
        held = look_up(as_row(held), held)
    held_row = as_row(held)
    same = p_row == p_col
    before = last(same & earlier)
    source = jnp.where(before >= 0, look_up(held_row, before), p_col)
    leaves = look_up(held_row, last(same))
    owner = source // rows_dev
    slot = jnp.sum(
        jnp.where((as_row(owner) == owner) & earlier, 1, 0), axis=1, keepdims=True
    )
    code = owner * slots + jnp.minimum(slot, slots - 1)
    mine = (owner == me) & (slot == over)
    offset = source - me * rows_dev
    wide = lax.broadcasted_iota(jnp.int32, (NB, PROWS * slots), 1)
    code_wide = owner * slots + slot
    hit = (code_wide == wide) & (slot < slots)
    table[pl.ds(0, 1), pl.ds(0, NB)] = as_row(code)
    table[pl.ds(1, 1), pl.ds(0, NB)] = jnp.sum(
        jnp.where(mine, offset, 0), axis=0, keepdims=True
    )
    table[pl.ds(3, 1), :] = jnp.sum(jnp.where(hit, leaves, 0), axis=0, keepdims=True)
    note[pl.ds(0, 1), :] = table[pl.ds(1, 1), pl.ds(0, NB)]
    note[pl.ds(1, 1), :] = jnp.broadcast_to(
        jnp.sum(jnp.where(owner == me, 1, 0), axis=0, keepdims=True), (1, NB)
    )
    most[...] = jnp.broadcast_to(jnp.max(as_row(slot), axis=1, keepdims=True), (1, NB))


def exchange_kernel(
    slots,
    pivots_hbm, matrix,
    resident, gathered, panel, inverse, returned, note, most,
    pivots, table, plan, picks, received, ordered, top, top_a, top_b, back, corner,
    row_send, row_recv, ret_send, ret_recv, ring_send, ring_recv,
    top_send, top_recv, panel_send, panel_recv, low_send, low_recv, own_sem, load_sem,
):
    half = NB // 2
    rows_dev = matrix.shape[0]
    me = lax.axis_index("prow")
    col = lax.axis_index("pcol")
    x, y = me // SIDE, me % SIDE
    z, core = col // 2, col % 2
    sent = []

    def block(q):
        return pl.ds(pl.multiple_of(q * NB, NB), NB)

    def remote(src, dst, send_sem, recv_sem, device):
        return pltpu.make_async_remote_copy(
            src_ref=src, dst_ref=dst, send_sem=send_sem, recv_sem=recv_sem, device_id=device
        )

    def ahead(d):
        return jnp.where(me + d >= PROWS, me + d - PROWS, me + d)

    def behind(d):
        return jnp.where(me >= d, me - d, me - d + PROWS)

    z_up = jnp.where(col >= 6, col - 6, col + 2)
    z_down = jnp.where(col >= 2, col - 2, col + 6)
    other = jnp.where(core == 0, col + 1, col - 1)
    pivots_in = pltpu.make_async_copy(pivots_hbm, pivots, own_sem.at[10])
    pivots_in.start()
    loads = []
    for k in range(LOADS):
        part = pl.ds(k * (rows_dev // LOADS), rows_dev // LOADS)
        loads.append(
            pltpu.make_async_copy(matrix.at[part, :], resident.at[part, :], load_sem.at[k])
        )
        loads[-1].start()
    barrier = pltpu.get_barrier_semaphore()
    for d in range(1, PROWS):
        pl.semaphore_signal(barrier, inc=1, device_id={"prow": ahead(d)})
    for c in (z_up, z_down, other):
        pl.semaphore_signal(barrier, inc=1, device_id={"pcol": c})
    pl.semaphore_wait(barrier, PROWS - 1 + 3)

    def top_x(d):
        return remote(
            resident.at[pl.ds(0, half), pl.ds(d * SIDE * NB, SIDE * NB)], top_a,
            top_send.at[d], top_recv.at[0], {"prow": d * SIDE},
        )

    def top_y(d, k):
        return remote(
            resident.at[pl.ds(half, half), pl.ds((k * SIDE + d) * NB, NB)],
            top_b.at[:, pl.ds(k * NB, NB)],
            top_send.at[4 + 4 * d + k], top_recv.at[1 + k], {"prow": d},
        )

    loads[0].wait()

    @pl.when(me == 0)
    def _():
        for d in (1, 3, 2):
            top_x(d).start()
            for k in range(SIDE):
                top_y(d, k).start()
        top_a[...] = resident[pl.ds(0, half), pl.ds(0, SIDE * NB)]
        for k in range(SIDE):
            top_b[:, pl.ds(k * NB, NB)] = resident[pl.ds(half, half), pl.ds(k * SIDE * NB, NB)]


    def low_copy(k, device):
        return remote(corner, corner, low_send.at[k], low_recv.at[0], device)

    def low_sends(act):
        @pl.when(me == 0)
        def _():
            @pl.when(core == 0)
            def _():
                act(low_copy(0, {"pcol": other}))

                @pl.when(z <= 1)
                def _():
                    act(low_copy(1, {"pcol": z_up}))

                @pl.when(z == 0)
                def _():
                    act(low_copy(2, {"pcol": z_down}))

            for d in (2, 1, 3):
                act(low_copy(2 + d, {"prow": d * SIDE}))

    def low_sends_y(act):
        @pl.when(y == 0)
        def _():
            for d in (2, 1, 3):
                act(low_copy(5 + d, {"prow": x * SIDE + d}))

    @pl.when((me == 0) & (col == 0))
    def _():
        corner[...] = resident[pl.ds(0, NB), pl.ds(0, NB)]
        low_sends(lambda c: c.start())

    halves = [pl.ds(0, rows_dev // 2), pl.ds(rows_dev // 2, rows_dev // 2)]
    first_panel = matrix.at[:, pl.ds(0, NB)]

    def panel_first(h, k, to):
        return remote(
            first_panel.at[halves[h]], panel.at[halves[h]],
            panel_send.at[k], panel_recv.at[h], {"pcol": to},
        )

    def panel_next(h, k, to):
        return remote(
            panel.at[halves[h]], panel.at[halves[h]],
            panel_send.at[k], panel_recv.at[h], {"pcol": to},
        )

    panel_own = pltpu.make_async_copy(first_panel, panel, own_sem.at[7])

    @pl.when(col == 0)
    def _():
        panel_first(0, 0, z_up).start()
        panel_first(1, 1, z_down).start()
        panel_first(1, 2, z_up).start()
        panel_first(0, 3, z_down).start()
        panel_first(0, 4, other).start()
        panel_first(1, 5, other).start()
        panel_own.start()

    pivots_in.wait()
    swap_plan(slots, pivots, me, rows_dev, table, note, most)
    plan_copy = pltpu.make_async_copy(table, plan, own_sem.at[9])
    plan_copy.start()
    plan_copy.wait()
    for c in loads[1:]:
        c.wait()

    def pick(s, carry):
        row = resident[pl.ds(plan[1, s], 1), :]
        for q in range(PROWS):
            picks[pl.ds(q * slots + s, 1), :] = row[:, q * NB : (q + 1) * NB]
        return carry

    lax.fori_loop(0, slots, pick, 0)

    def row_copy(d):
        peer = ahead(d)
        return remote(
            picks.at[pl.ds(pl.multiple_of(peer * slots, 8), slots)],
            received.at[pl.ds(pl.multiple_of(me * slots, 8), slots)],
            row_send.at[d], row_recv.at[d], {"prow": peer},
        )

    def row_start(d, carry):
        row_copy(d).start()
        return carry

    def row_wait(d, carry):
        row_copy(d).wait_recv()
        return carry

    def row_sent(d, carry):
        row_copy(d).wait_send()
        return carry

    for d in (10, 2, 8, 6, 9, 7, 11, 5, 13, 3, 14, 1, 15, 4, 12):
        row_start(d, 0)

    mine = pl.ds(pl.multiple_of(me * slots, 8), slots)
    received[mine, :] = picks[mine, :]

    @pl.when((me == 0) & (col != 0))
    def _():
        low_copy(0, {"pcol": other}).wait_recv()
        low_sends(lambda c: c.start())

    def panel_leg(h, there):
        @pl.when((core == 0) & there)
        def _():
            panel_next(h, 0, other).wait_recv()
            panel_next(h, 4 + h, other).start()

            @pl.when((z == 1) if h == 0 else (z == 3))
            def _():
                panel_next(h, 0, 4).start()

    for h in (0, 1):
        panel_leg(h, z == 1 if h == 0 else z == 3)
    for h in (0, 1):
        panel_leg(h, z == 3 if h == 0 else z == 1)

    lax.fori_loop(1, PROWS, row_wait, 0)

    def order(j, carry):
        ordered[pl.ds(j, 1), :] = received[pl.ds(plan[0, j], 1), :]
        return carry

    lax.fori_loop(0, NB, order, 0, unroll=8)
    gathered[:, block(me)] = ordered[...]

    def spot(o, along, across):
        dx, dy = (along, across) if o == 0 else (across, along)
        xx, yy = x + dx, y + dy
        if dx:
            xx = jnp.where(xx >= SIDE, xx - SIDE, jnp.where(xx < 0, xx + SIDE, xx))
        if dy:
            yy = jnp.where(yy >= SIDE, yy - SIDE, jnp.where(yy < 0, yy + SIDE, yy))
        return xx * SIDE + yy

    def ring_copy(o, q, sem, device):
        ref = gathered.at[pl.ds(o * half, half), block(q)]
        return remote(ref, ref, ring_send.at[o, sem], ring_recv.at[o, sem], {"prow": device})

    def ring_start(o, q, sem, device):
        c = ring_copy(o, q, sem, device)
        c.start()
        sent.append(c)

    for d in (2, 1, 3):
        for o in (0, 1):
            ring_start(o, me, d, spot(o, d, 0))
    for d in (2, 1, 3):
        for o in (0, 1):
            ring_start(o, me, 3 + d, spot(o, 0, d))

    def top_leg(a, d):
        if a == 0:
            src, dst, device = top_a, top.at[pl.ds(0, half)], x * SIDE + d
        else:
            src, dst, device = top_b, top.at[pl.ds(half, half)], d * SIDE + y
        return remote(
            src.at[:, pl.ds(d * NB, NB)], dst,
            top_send.at[20 + 4 * a + d], top_recv.at[5 + a], {"prow": device},
        )

    @pl.when(y == 0)
    def _():
        @pl.when(x != 0)
        def _():
            top_x(1).wait_recv()

        for d in range(1, SIDE):
            top_leg(0, d).start()
        top[pl.ds(0, half), :] = top_a[:, pl.ds(0, NB)]

    @pl.when(x == 0)
    def _():
        @pl.when(y != 0)
        def _():
            for k in range(SIDE):
                top_y(1, k).wait_recv()

        for d in range(1, SIDE):
            top_leg(1, d).start()
        top[pl.ds(half, half), :] = top_b[:, pl.ds(0, NB)]

    @pl.when(y == 0)
    def _():
        @pl.when(x != 0)
        def _():
            low_copy(0, {"pcol": other}).wait_recv()

    low_sends_y(lambda c: c.start())

    for e in (1, 3, 2):
        for o in (0, 1):
            q = spot(o, -e, 0)
            ring_copy(o, q, e, me).wait_recv()
            for d in (2, 1, 3):
                ring_start(o, q, 3 + 3 * e + d, spot(o, 0, d))

    panel_leg(0, z == 2)
    panel_leg(1, z == 2)

    @pl.when(y != 0)
    def _():
        top_leg(0, 1).wait_recv()

    @pl.when(x != 0)
    def _():
        top_leg(1, 1).wait_recv()

    def back_rows(r, carry):
        for s in range(slots):
            index = plan[3, r * slots + s]
            back[pl.ds(r * slots + s, 1), :] = top[pl.ds(index, 1), :]
        return carry

    lax.fori_loop(0, PROWS, back_rows, 0)

    def ret_copy(d):
        peer = ahead(d)
        return remote(
            back.at[pl.ds(pl.multiple_of(peer * slots, 8), slots)],
            returned.at[:, block(me)],
            ret_send.at[d], ret_recv.at[d], {"prow": peer},
        )

    def ret_start(d, carry):
        ret_copy(d).start()
        return carry

    def ret_wait(d, carry):
        peer = behind(d)
        remote(
            back.at[pl.ds(0, slots)], returned.at[:, block(peer)],
            ret_send.at[d], ret_recv.at[d], {"prow": peer},
        ).wait_recv()
        return carry

    def ret_sent(d, carry):
        ret_copy(d).wait_send()
        return carry

    lax.fori_loop(1, PROWS, ret_start, 0)
    ret_own = pltpu.make_async_copy(
        back.at[pl.ds(pl.multiple_of(me * slots, 8), slots)],
        returned.at[:, block(me)], own_sem.at[8],
    )
    ret_own.start()

    @pl.when(y != 0)
    def _():
        low_copy(0, {"pcol": other}).wait_recv()

    inverse[...] = invert_unit_lower(corner[...])

    for e in (0, 1, 3, 2):
        for d in (1, 3, 2):
            for o in (0, 1):
                ring_copy(o, spot(o, -e, -d), 3 + 3 * e + d, me).wait_recv()

    lax.fori_loop(1, PROWS, ret_wait, 0)
    ret_own.wait()

    @pl.when(core == 1)
    def _():
        panel_next(0, 0, other).wait_recv()
        panel_next(1, 0, other).wait_recv()

    for c in sent:
        c.wait_send()
    lax.fori_loop(1, PROWS, row_sent, 0)
    lax.fori_loop(1, PROWS, ret_sent, 0)

    @pl.when(me == 0)
    def _():
        for d in (1, 3, 2):
            top_x(d).wait_send()
            for k in range(SIDE):
                top_y(d, k).wait_send()

    @pl.when(y == 0)
    def _():
        for d in range(1, SIDE):
            top_leg(0, d).wait_send()

    @pl.when(x == 0)
    def _():
        for d in range(1, SIDE):
            top_leg(1, d).wait_send()

    @pl.when(col == 0)
    def _():
        panel_own.wait()
        for h, k in ((0, 0), (1, 1), (1, 2), (0, 3), (0, 4), (1, 5)):
            panel_first(h, k, other).wait_send()

    low_sends(lambda c: c.wait_send())
    low_sends_y(lambda c: c.wait_send())

    @pl.when((core == 0) & (z > 0))
    def _():
        panel_next(0, 4, other).wait_send()
        panel_next(1, 5, other).wait_send()

        @pl.when(z == 1)
        def _():
            panel_next(0, 0, other).wait_send()

        @pl.when(z == 3)
        def _():
            panel_next(1, 0, other).wait_send()


def exchange(slots, collective_id, matrix, pivots):
    rows_dev, cols_dev = matrix.shape
    f32, i32 = jnp.float32, jnp.int32
    vmem = pl.BlockSpec(memory_space=pltpu.VMEM)
    hbm = pl.BlockSpec(memory_space=pltpu.HBM)
    dma = pltpu.SemaphoreType.DMA
    return pl.pallas_call(
        functools.partial(exchange_kernel, slots),
        out_shape=[
            pltpu.VMEM((rows_dev, cols_dev), f32),
            jax.ShapeDtypeStruct((NB, cols_dev), f32),
            jax.ShapeDtypeStruct((rows_dev, NB), f32),
            jax.ShapeDtypeStruct((NB, NB), f32),
            jax.ShapeDtypeStruct((slots, cols_dev), f32),
            jax.ShapeDtypeStruct((2, NB), i32),
            jax.ShapeDtypeStruct((1, NB), i32),
        ],
        in_specs=[hbm, hbm],
        out_specs=[vmem] * 7,
        scratch_shapes=[
            pltpu.VMEM((1, NB), i32),
            pltpu.VMEM((8, PROWS * slots), i32),
            pltpu.SMEM((8, PROWS * slots), i32),
            pltpu.VMEM((PROWS * slots, NB), f32),
            pltpu.VMEM((PROWS * slots, NB), f32),
            pltpu.VMEM((NB, NB), f32),
            pltpu.VMEM((NB, NB), f32),
            pltpu.VMEM((NB // 2, SIDE * NB), f32),
            pltpu.VMEM((NB // 2, SIDE * NB), f32),
            pltpu.VMEM((PROWS * slots, NB), f32),
            pltpu.VMEM((NB, NB), f32),
            dma((PROWS,)), dma((PROWS,)), dma((PROWS,)), dma((PROWS,)),
            dma((2, 16)), dma((2, 16)),
            dma((28,)), dma((7,)), dma((6,)), dma((2,)), dma((10,)), dma((1,)), dma((11,)),
            dma((LOADS,)),
        ],
        compiler_params=pltpu.CompilerParams(
            collective_id=collective_id, has_side_effects=True, vmem_limit_bytes=24 * MIB
        ),
        name="exchange_%d" % slots,
    )(pivots, pltpu.with_memory_space_constraint(matrix, pltpu.HBM))


def split(value):
    high = value.astype(jnp.bfloat16)
    return high, (value - high.astype(jnp.float32)).astype(jnp.bfloat16)


def stacked(value):
    high, low = split(value)
    return jnp.concatenate([high, low, high], axis=1)


def update_kernel(
    note, block, gathered, panel, inverse, returned, out, matrix,
    notes, result, factor, note_sem, sems,
):
    me = lax.axis_index("prow")
    col = lax.axis_index("pcol")
    note_copy = pltpu.make_async_copy(note, notes, note_sem.at[0])
    note_copy.start()
    factor[...] = stacked(panel[...])
    solve = stacked(inverse[...])
    note_copy.wait()

    def replace(s, carry):
        matrix[pl.ds(notes[0, s], 1), :] = returned[pl.ds(s, 1), :]
        return carry

    lax.fori_loop(0, notes[1, 0], replace, 0)

    def write(n):
        return pltpu.make_async_copy(
            result.at[:, pl.ds(n * WIDE, WIDE)], out.at[:, pl.ds(n * WIDE, WIDE)], sems.at[n]
        )

    def terms(value):
        high, low = split(value)
        return jnp.concatenate([high, high, low], axis=0)

    rows = matrix.shape[0] - NB
    parts = matrix.shape[1] // WIDE
    for n in range(parts):
        here = pl.ds(n * WIDE, WIDE)
        upper = jnp.dot(solve, terms(gathered[:, here]), preferred_element_type=jnp.float32)
        value = matrix[:, here] - jnp.dot(
            factor[...], terms(upper), preferred_element_type=jnp.float32
        )
        head = jnp.where(me == 0, upper, value[:NB])
        if n == 0:
            keep = col == 0
            result[pl.ds(0, NB), pl.ds(0, NB)] = jnp.where(keep, panel[pl.ds(0, NB), :], head[:, :NB])
            result[pl.ds(NB, rows), pl.ds(0, NB)] = jnp.where(
                keep, panel[pl.ds(NB, rows), :], value[NB:, :NB]
            )
            result[pl.ds(0, NB), pl.ds(NB, WIDE - NB)] = head[:, NB:]
            result[pl.ds(NB, rows), pl.ds(NB, WIDE - NB)] = value[NB:, NB:]
        else:
            result[pl.ds(0, NB), here] = head
            result[pl.ds(NB, rows), here] = value[NB:]

        write(n).start()
    for n in range(parts):
        write(n).wait()


def update(matrix, gathered, panel, inverse, returned, note):
    rows_dev, cols_dev = matrix.shape
    vmem = pl.BlockSpec(memory_space=pltpu.VMEM)
    out, _ = pl.pallas_call(
        update_kernel,
        out_shape=[
            pltpu.HBM(matrix.shape, jnp.float32), pltpu.VMEM(matrix.shape, jnp.float32)
        ],
        in_specs=[vmem] * 6,
        out_specs=[pl.BlockSpec(memory_space=pltpu.HBM), vmem],
        input_output_aliases={1: 1},
        scratch_shapes=[
            pltpu.SMEM((2, NB), jnp.int32),
            pltpu.VMEM((rows_dev, cols_dev), jnp.float32),
            pltpu.VMEM((rows_dev, 3 * NB), jnp.bfloat16),
            pltpu.SemaphoreType.DMA((1,)),
            pltpu.SemaphoreType.DMA((cols_dev // WIDE,)),
        ],
        compiler_params=pltpu.CompilerParams(vmem_limit_bytes=28 * MIB),
        name="update",
    )(note, matrix, gathered, panel, inverse, returned)
    return out


def local(matrix, pivots):
    pivots = pivots.reshape(1, NB)
    *found, most = exchange(FEW, 0, matrix, pivots)

    def many():
        *found, _ = exchange(NB, 1, matrix, pivots)
        return update(*found)

    return lax.cond(most[0, 0] < FEW, lambda: update(*found), many)


def solution(mesh):
    placed = (P("prow", "pcol"), P())
    return jax.shard_map(
        local, mesh=mesh, in_specs=placed, out_specs=P("prow", "pcol"), check_vma=False
    )
```

```python
import functools

import jax
import jax.numpy as jnp
from jax import lax
from jax.experimental import pallas as pl
from jax.experimental.pallas import tpu as pltpu
from jax.sharding import PartitionSpec as P

NB = 128
PROWS = 16
SIDE = 4
FEW = 24
MIB = 1024 * 1024
LOADS = 8
WIDE = 256
HIGHEST = lax.Precision.HIGHEST


def invert_unit_lower(block):
    rows = lax.broadcasted_iota(jnp.int32, (NB, NB), 0)
    cols = lax.broadcasted_iota(jnp.int32, (NB, NB), 1)
    eye = jnp.where(rows == cols, 1.0, 0.0).astype(jnp.float32)
    dot = functools.partial(jnp.dot, precision=HIGHEST, preferred_element_type=jnp.float32)
    inverse = eye
    size = 1
    while size < NB:
        corner = (rows // size == cols // size + 1) & (rows // (2 * size) == cols // (2 * size))
        part = jnp.where(corner, block, 0.0)
        if size == 1:
            inverse = eye - part
        else:
            inverse = inverse - dot(dot(inverse, part), inverse)
        size *= 2
    return inverse


def swap_plan(slots, pivots, me, rows_dev, table, note, most):
    shape = (NB, NB)
    down = lax.broadcasted_iota(jnp.int32, shape, 0)
    over = lax.broadcasted_iota(jnp.int32, shape, 1)
    earlier, later = over < down, down < over

    def by_row(value):
        return jnp.sum(value, axis=1, keepdims=True)

    def by_column(value):
        return jnp.sum(value, axis=0, keepdims=True)

    def look_up(vector, index):
        column, row = vector
        at_column, at_row = index
        return (
            by_row(jnp.where(over == at_column, row, 0)),
            by_column(jnp.where(down == at_row, column, 0)),
        )

    def last(where, where_t):
        return (
            jnp.max(jnp.where(where, over, -1), axis=1, keepdims=True),
            jnp.max(jnp.where(where_t, down, -1), axis=0, keepdims=True),
        )

    def choose(index, yes, no):
        return tuple(jnp.where(i >= 0, a, b) for i, a, b in zip(index, yes, no))

    p_row = pivots[...]
    p = by_row(jnp.where(down == over, p_row, 0)), p_row
    steps = (
        lax.broadcasted_iota(jnp.int32, (NB, 1), 0), lax.broadcasted_iota(jnp.int32, (1, NB), 1)
    )
    touched = last((p[1] == down) & earlier, (p[0] == over) & later)
    held = choose(touched, touched, steps)
    for _ in range(7):
        held = look_up(held, held)
    same = p[0] == p[1]
    before = last(same & earlier, same & later)
    source = choose(before, look_up(held, before), p)
    owner = tuple(v // rows_dev for v in source)
    alike = owner[0] == owner[1]
    slot = (
        by_row(jnp.where(alike & earlier, 1, 0)), by_column(jnp.where(alike & later, 1, 0))
    )
    offset = source[0] - me * rows_dev
    mine = (owner[0] == me) & (slot[0] == over)
    picked = by_column(jnp.where(mine, offset, 0))
    table[pl.ds(0, 1), pl.ds(0, NB)] = owner[1] * slots + jnp.minimum(slot[1], slots - 1)
    table[pl.ds(1, 1), pl.ds(0, NB)] = picked
    leaves = look_up(held, last(same, same))[0]
    wide = lax.broadcasted_iota(jnp.int32, (NB, PROWS * slots), 1)
    hit = (owner[0] * slots + slot[0] == wide) & (slot[0] < slots)
    table[pl.ds(3, 1), :] = by_column(jnp.where(hit, leaves, 0))
    note[pl.ds(0, 1), :] = picked
    note[pl.ds(1, 1), :] = jnp.broadcast_to(
        by_column(jnp.where(owner[0] == me, 1, 0)), (1, NB)
    )
    most[...] = jnp.broadcast_to(by_row(jnp.max(slot[0], axis=0, keepdims=True)), (1, NB))


def exchange_kernel(
    slots,
    pivots_hbm, matrix,
    resident, gathered, panel, inverse, returned, note, most,
    pivots, table, plan, picks, received, ordered, top, top_a, top_b, back, corner,
    row_send, row_recv, ret_send, ret_recv, ring_send, ring_recv,
    top_send, top_recv, panel_send, panel_recv, low_send, low_recv, own_sem, load_sem,
):
    half = NB // 2
    rows_dev = matrix.shape[0]
    me = lax.axis_index("prow")
    col = lax.axis_index("pcol")
    x, y = me // SIDE, me % SIDE
    z, core = col // 2, col % 2

    def block(q):
        return pl.ds(pl.multiple_of(q * NB, NB), NB)

    def remote(src, dst, send_sem, recv_sem, device):
        return pltpu.make_async_remote_copy(
            src_ref=src, dst_ref=dst, send_sem=send_sem, recv_sem=recv_sem, device_id=device
        )

    def ahead(d):
        return jnp.where(me + d >= PROWS, me + d - PROWS, me + d)

    def behind(d):
        return jnp.where(me >= d, me - d, me - d + PROWS)

    z_up = jnp.where(col >= 6, col - 6, col + 2)
    z_down = jnp.where(col >= 2, col - 2, col + 6)
    other = jnp.where(core == 0, col + 1, col - 1)
    pivots_in = pltpu.make_async_copy(pivots_hbm, pivots, own_sem.at[10])
    pivots_in.start()
    panel_in = pltpu.make_async_copy(matrix.at[:, pl.ds(0, NB)], panel, own_sem.at[7])

    @pl.when(col == 0)
    def _():
        panel_in.start()

    loads = []
    for k in range(LOADS):
        part = pl.ds(k * (rows_dev // LOADS), rows_dev // LOADS)
        loads.append(
            pltpu.make_async_copy(matrix.at[part, :], resident.at[part, :], load_sem.at[k])
        )
        loads[-1].start()
    barrier = pltpu.get_barrier_semaphore()
    for d in range(1, PROWS):
        pl.semaphore_signal(barrier, inc=1, device_id={"prow": ahead(d)})
    for c in (z_up, z_down, other):
        pl.semaphore_signal(barrier, inc=1, device_id={"pcol": c})
    pl.semaphore_wait(barrier, PROWS - 1 + 3)

    def top_x(d):
        return remote(
            resident.at[pl.ds(0, half), pl.ds(d * SIDE * NB, SIDE * NB)], top_a,
            top_send.at[0], top_recv.at[0], {"prow": d * SIDE},
        )

    def top_y(d, k):
        return remote(
            resident.at[pl.ds(half, half), pl.ds((k * SIDE + d) * NB, NB)],
            top_b.at[:, pl.ds(k * NB, NB)],
            top_send.at[0], top_recv.at[1], {"prow": d},
        )

    loads[0].wait()

    @pl.when(me == 0)
    def _():
        for d in (1, 3, 2):
            top_x(d).start()
            for k in range(SIDE):
                top_y(d, k).start()
        top_a[...] = resident[pl.ds(0, half), pl.ds(0, SIDE * NB)]
        for k in range(SIDE):
            top_b[:, pl.ds(k * NB, NB)] = resident[pl.ds(half, half), pl.ds(k * SIDE * NB, NB)]

    def low_copy(k, device):
        return remote(corner, corner, low_send.at[k], low_recv.at[0], device)

    def low_sends(act):
        @pl.when(me == 0)
        def _():
            @pl.when(core == 0)
            def _():
                act(low_copy(0, {"pcol": other}))

                @pl.when(z <= 1)
                def _():
                    act(low_copy(1, {"pcol": z_up}))

                @pl.when(z == 0)
                def _():
                    act(low_copy(2, {"pcol": z_down}))

            for d in (2, 1, 3):
                act(low_copy(2 + d, {"prow": d * SIDE}))

    def low_sends_y(act):
        @pl.when(y == 0)
        def _():
            for d in (2, 1, 3):
                act(low_copy(5 + d, {"prow": x * SIDE + d}))

    @pl.when((me == 0) & (col == 0))
    def _():
        corner[...] = resident[pl.ds(0, NB), pl.ds(0, NB)]
        low_sends(lambda c: c.start())

    def panel_copy(h, k, to):
        ref = panel.at[pl.ds(pl.multiple_of(h * (rows_dev // 2), 8), rows_dev // 2)]
        return remote(ref, ref, panel_send.at[k], panel_recv.at[h], {"pcol": to})

    @pl.when(col == 0)
    def _():
        panel_in.wait()
        panel_copy(1, 2, other).start()
        panel_copy(0, 0, z_up).start()
        panel_copy(0, 1, z_down).start()
        panel_copy(0, 3, other).start()

    pivots_in.wait()
    swap_plan(slots, pivots, me, rows_dev, table, note, most)
    plan_copy = pltpu.make_async_copy(table, plan, own_sem.at[9])
    plan_copy.start()
    plan_copy.wait()
    for c in loads[1:]:
        c.wait()

    def pick(s, carry):
        row = resident[pl.ds(plan[1, s], 1), :]
        for q in range(PROWS):
            picks[pl.ds(q * slots + s, 1), :] = row[:, q * NB : (q + 1) * NB]
        return carry

    lax.fori_loop(0, slots, pick, 0)

    def row_copy(d):
        peer = ahead(d)
        return remote(
            picks.at[pl.ds(pl.multiple_of(peer * slots, 8), slots)],
            received.at[pl.ds(pl.multiple_of(me * slots, 8), slots)],
            row_send.at[0], row_recv.at[0], {"prow": peer},
        )

    def row_all():
        ref = received.at[pl.ds(0, (PROWS - 1) * slots)]
        return remote(ref, ref, row_send.at[0], row_recv.at[0], {"prow": ahead(1)})

    for d in (10, 2, 8, 6, 9, 7, 11, 5, 13, 3, 14, 1, 15, 4, 12):
        row_copy(d).start()

    mine = pl.ds(pl.multiple_of(me * slots, 8), slots)
    received[mine, :] = picks[mine, :]

    @pl.when((me == 0) & (col != 0))
    def _():
        low_copy(0, {"pcol": other}).wait_recv()
        low_sends(lambda c: c.start())

    def panel_leg():
        panel_copy(core, 0, other).wait_recv()

        @pl.when(z > 0)
        def _():
            panel_copy(core, 2, other).start()

        @pl.when((z == 0) | (z == 1 + 2 * core))
        def _():
            panel_copy(core, 0, jnp.where(z == 3, z_down, z_up)).start()

        @pl.when(z == 0)
        def _():
            panel_copy(core, 1, z_down).start()

    @pl.when((z != 2) & (col != 0))
    def _():
        panel_leg()

    def top_leg(a, d):
        if a == 0:
            src, dst, device = top_a, top.at[pl.ds(0, half)], x * SIDE + d
        else:
            src, dst, device = top_b, top.at[pl.ds(half, half)], d * SIDE + y
        return remote(
            src.at[:, pl.ds(d * NB, NB)], dst,
            top_send.at[1 + a], top_recv.at[2 + a], {"prow": device},
        )

    @pl.when(y == 0)
    def _():
        @pl.when(x != 0)
        def _():
            top_x(1).wait_recv()

        for d in range(1, SIDE):
            top_leg(0, d).start()
        top[pl.ds(0, half), :] = top_a[:, pl.ds(0, NB)]

    @pl.when(x == 0)
    def _():
        @pl.when(y != 0)
        def _():
            remote(top_b, top_b, top_send.at[0], top_recv.at[1], {"prow": 1}).wait_recv()

        for d in range(1, SIDE):
            top_leg(1, d).start()
        top[pl.ds(half, half), :] = top_b[:, pl.ds(0, NB)]

    row_all().wait_recv()

    def order(j, carry):
        ordered[pl.ds(j, 1), :] = received[pl.ds(plan[0, j], 1), :]
        return carry

    lax.fori_loop(0, NB, order, 0, unroll=8)
    gathered[:, block(me)] = ordered[...]

    def spot(o, along, across):
        dx, dy = (along, across) if o == 0 else (across, along)
        xx, yy = x + dx, y + dy
        if dx:
            xx = jnp.where(xx >= SIDE, xx - SIDE, jnp.where(xx < 0, xx + SIDE, xx))
        if dy:
            yy = jnp.where(yy >= SIDE, yy - SIDE, jnp.where(yy < 0, yy + SIDE, yy))
        return xx * SIDE + yy

    def ring_copy(o, q, sem, device):
        ref = gathered.at[pl.ds(o * half, half), block(q)]
        return remote(ref, ref, ring_send.at[0], ring_recv.at[sem], {"prow": device})

    def ring_all(blocks, sem):
        ref = gathered.at[:, pl.ds(0, blocks * NB)]
        return remote(ref, ref, ring_send.at[0], ring_recv.at[sem], {"prow": ahead(1)})

    def ring_start(o, q, sem, device):
        ring_copy(o, q, sem, device).start()

    for d in (2, 1, 3):
        for o in (0, 1):
            ring_start(o, me, 2 * d + o - 1, spot(o, d, 0))
    for d in (2, 1, 3):
        for o in (0, 1):
            ring_start(o, me, 0, spot(o, 0, d))

    @pl.when(y == 0)
    def _():
        @pl.when(x != 0)
        def _():
            low_copy(0, {"pcol": other}).wait_recv()

    low_sends_y(lambda c: c.start())

    @pl.when(y != 0)
    def _():
        top_leg(0, 1).wait_recv()

    @pl.when(x != 0)
    def _():
        top_leg(1, 1).wait_recv()

    def back_rows(r, carry):
        for s in range(slots):
            index = plan[3, r * slots + s]
            back[pl.ds(r * slots + s, 1), :] = top[pl.ds(index, 1), :]
        return carry

    lax.fori_loop(0, PROWS, back_rows, 0)

    def ret_copy(d):
        peer = ahead(d)
        return remote(
            back.at[pl.ds(pl.multiple_of(peer * slots, 8), slots)],
            returned.at[:, block(me)],
            ret_send.at[0], ret_recv.at[0], {"prow": peer},
        )

    def ret_all():
        ref = returned.at[:, pl.ds(0, (PROWS - 1) * NB)]
        return remote(ref, ref, ret_send.at[0], ret_recv.at[0], {"prow": ahead(1)})

    for d in (10, 2, 8, 6, 9, 7, 11, 5, 13, 3, 14, 1, 15, 4, 12):
        ret_copy(d).start()
    ret_own = pltpu.make_async_copy(
        back.at[pl.ds(pl.multiple_of(me * slots, 8), slots)],
        returned.at[:, block(me)], own_sem.at[8],
    )
    ret_own.start()

    for e in (1, 3, 2):
        for o in (0, 1):
            q = spot(o, -e, 0)
            ring_copy(o, q, 2 * e + o - 1, me).wait_recv()
            for d in (2, 1, 3):
                ring_start(o, q, 0, spot(o, 0, d))

    @pl.when(z == 2)
    def _():
        panel_leg()

    @pl.when(y != 0)
    def _():
        low_copy(0, {"pcol": other}).wait_recv()

    inverse[...] = invert_unit_lower(corner[...])

    ring_all(12, 0).wait_recv()
    ret_all().wait_recv()
    ret_own.wait()

    @pl.when(col != 0)
    def _():
        panel_copy(1 - core, 0, other).wait_recv()

    ring_all(15, 0).wait_send()
    row_all().wait_send()
    ret_all().wait_send()

    @pl.when(me == 0)
    def _():
        ref = resident.at[pl.ds(0, NB), pl.ds(0, 12 * NB)]
        remote(ref, ref, top_send.at[0], top_recv.at[0], {"prow": 1}).wait_send()

    @pl.when(y == 0)
    def _():
        ref = top_a.at[:, pl.ds(0, 3 * NB)]
        remote(ref, ref, top_send.at[1], top_recv.at[2], {"prow": 1}).wait_send()

    @pl.when(x == 0)
    def _():
        ref = top_b.at[:, pl.ds(0, 3 * NB)]
        remote(ref, ref, top_send.at[2], top_recv.at[3], {"prow": 1}).wait_send()

    @pl.when(col == 0)
    def _():
        panel_copy(0, 3, other).wait_send()

    @pl.when((z > 0) | (core == 0))
    def _():
        panel_copy(core, 2, other).wait_send()

    @pl.when((z == 0) | (z == 1 + 2 * core))
    def _():
        panel_copy(core, 0, other).wait_send()

    @pl.when(z == 0)
    def _():
        panel_copy(core, 1, other).wait_send()

    low_sends(lambda c: c.wait_send())
    low_sends_y(lambda c: c.wait_send())


def exchange(slots, collective_id, matrix, pivots):
    rows_dev, cols_dev = matrix.shape
    f32, i32 = jnp.float32, jnp.int32
    vmem = pl.BlockSpec(memory_space=pltpu.VMEM)
    hbm = pl.BlockSpec(memory_space=pltpu.HBM)
    dma = pltpu.SemaphoreType.DMA
    return pl.pallas_call(
        functools.partial(exchange_kernel, slots),
        out_shape=[
            pltpu.VMEM((rows_dev, cols_dev), f32),
            jax.ShapeDtypeStruct((NB, cols_dev), f32),
            jax.ShapeDtypeStruct((rows_dev, NB), f32),
            jax.ShapeDtypeStruct((NB, NB), f32),
            jax.ShapeDtypeStruct((slots, cols_dev), f32),
            jax.ShapeDtypeStruct((2, NB), i32),
            jax.ShapeDtypeStruct((1, NB), i32),
        ],
        in_specs=[hbm, hbm],
        out_specs=[vmem] * 7,
        scratch_shapes=[
            pltpu.VMEM((1, NB), i32),
            pltpu.VMEM((8, PROWS * slots), i32),
            pltpu.SMEM((8, PROWS * slots), i32),
            pltpu.VMEM((PROWS * slots, NB), f32),
            pltpu.VMEM((PROWS * slots, NB), f32),
            pltpu.VMEM((NB, NB), f32),
            pltpu.VMEM((NB, NB), f32),
            pltpu.VMEM((NB // 2, SIDE * NB), f32),
            pltpu.VMEM((NB // 2, SIDE * NB), f32),
            pltpu.VMEM((PROWS * slots, NB), f32),
            pltpu.VMEM((NB, NB), f32),
            dma((1,)), dma((1,)), dma((1,)), dma((1,)),
            dma((1,)), dma((7,)),
            dma((3,)), dma((4,)), dma((4,)), dma((2,)), dma((10,)), dma((1,)), dma((11,)),
            dma((LOADS,)),
        ],
        compiler_params=pltpu.CompilerParams(
            collective_id=collective_id, has_side_effects=True, vmem_limit_bytes=24 * MIB
        ),
        name="exchange_%d" % slots,
    )(pivots, pltpu.with_memory_space_constraint(matrix, pltpu.HBM))


def split(value):
    high = value.astype(jnp.bfloat16)
    return high, (value - high.astype(jnp.float32)).astype(jnp.bfloat16)


def stacked(value):
    high, low = split(value)
    return jnp.concatenate([high, low, high], axis=1)


def update_kernel(
    note, block, gathered, panel, inverse, returned, out, matrix,
    notes, result, factor, note_sem, sems,
):
    me = lax.axis_index("prow")
    col = lax.axis_index("pcol")
    note_copy = pltpu.make_async_copy(note, notes, note_sem.at[0])
    note_copy.start()
    factor[...] = stacked(panel[...])
    solve = stacked(inverse[...])
    note_copy.wait()

    def replace(s, carry):
        matrix[pl.ds(notes[0, s], 1), :] = returned[pl.ds(s, 1), :]
        return carry

    lax.fori_loop(0, notes[1, 0], replace, 0)

    def write(n):
        return pltpu.make_async_copy(
            result.at[:, pl.ds(n * WIDE, WIDE)], out.at[:, pl.ds(n * WIDE, WIDE)], sems.at[n]
        )

    def terms(value):
        high, low = split(value)
        return jnp.concatenate([high, high, low], axis=0)

    rows = matrix.shape[0] - NB
    parts = matrix.shape[1] // WIDE
    for n in range(parts):
        here = pl.ds(n * WIDE, WIDE)
        upper = jnp.dot(solve, terms(gathered[:, here]), preferred_element_type=jnp.float32)
        value = matrix[:, here] - jnp.dot(
            factor[...], terms(upper), preferred_element_type=jnp.float32
        )
        head = jnp.where(me == 0, upper, value[:NB])
        if n == 0:
            keep = col == 0
            result[pl.ds(0, NB), pl.ds(0, NB)] = jnp.where(keep, panel[pl.ds(0, NB), :], head[:, :NB])
            result[pl.ds(NB, rows), pl.ds(0, NB)] = jnp.where(
                keep, panel[pl.ds(NB, rows), :], value[NB:, :NB]
            )
            result[pl.ds(0, NB), pl.ds(NB, WIDE - NB)] = head[:, NB:]
            result[pl.ds(NB, rows), pl.ds(NB, WIDE - NB)] = value[NB:, NB:]
        else:
            result[pl.ds(0, NB), here] = head
            result[pl.ds(NB, rows), here] = value[NB:]

        write(n).start()
    for n in range(parts):
        write(n).wait()


def update(matrix, gathered, panel, inverse, returned, note):
    rows_dev, cols_dev = matrix.shape
    vmem = pl.BlockSpec(memory_space=pltpu.VMEM)
    out, _ = pl.pallas_call(
        update_kernel,
        out_shape=[
            pltpu.HBM(matrix.shape, jnp.float32), pltpu.VMEM(matrix.shape, jnp.float32)
        ],
        in_specs=[vmem] * 6,
        out_specs=[pl.BlockSpec(memory_space=pltpu.HBM), vmem],
        input_output_aliases={1: 1},
        scratch_shapes=[
            pltpu.SMEM((2, NB), jnp.int32),
            pltpu.VMEM((rows_dev, cols_dev), jnp.float32),
            pltpu.VMEM((rows_dev, 3 * NB), jnp.bfloat16),
            pltpu.SemaphoreType.DMA((1,)),
            pltpu.SemaphoreType.DMA((cols_dev // WIDE,)),
        ],
        compiler_params=pltpu.CompilerParams(vmem_limit_bytes=28 * MIB),
        name="update",
    )(note, matrix, gathered, panel, inverse, returned)
    return out


def local(matrix, pivots):
    pivots = pivots.reshape(1, NB)
    *found, most = exchange(FEW, 0, matrix, pivots)

    def many():
        *found, _ = exchange(NB, 1, matrix, pivots)
        return update(*found)

    return lax.cond(most[0, 0] < FEW, lambda: update(*found), many)


def solution(mesh):
    placed = (P("prow", "pcol"), P())
    return jax.shard_map(
        local, mesh=mesh, in_specs=placed, out_specs=P("prow", "pcol"), check_vma=False
    )
```

```python
import functools

import jax
import jax.numpy as jnp
from jax import lax
from jax.experimental import pallas as pl
from jax.experimental.pallas import tpu as pltpu
from jax.sharding import PartitionSpec as P

NB = 128
PROWS = 16
SIDE = 4
FEW = 24
MIB = 1024 * 1024
LOADS = 8
WIDE = 256


def split(value):
    high = value.astype(jnp.bfloat16)
    return high, (value - high.astype(jnp.float32)).astype(jnp.bfloat16)


def stacked(value):
    high, low = split(value)
    return jnp.concatenate([high, low, high], axis=1)


def terms(value):
    high, low = split(value)
    return jnp.concatenate([high, high, low], axis=0)


def dot_parts(left, right):
    return jnp.dot(stacked(left), terms(right), preferred_element_type=jnp.float32)


def invert_unit_lower(block):
    rows = lax.broadcasted_iota(jnp.int32, (NB, NB), 0)
    cols = lax.broadcasted_iota(jnp.int32, (NB, NB), 1)
    eye = jnp.where(rows == cols, 1.0, 0.0).astype(jnp.float32)
    inverse = eye
    size = 1
    while size < NB:
        corner = (rows // size == cols // size + 1) & (rows // (2 * size) == cols // (2 * size))
        part = jnp.where(corner, block, 0.0)
        if size == 1:
            inverse = eye - part
        else:
            inverse = inverse - dot_parts(dot_parts(inverse, part), inverse)
        size *= 2
    return inverse


def swap_plan(slots, pivots, me, rows_dev, table, note, most):
    shape = (NB, NB)
    down = lax.broadcasted_iota(jnp.int32, shape, 0)
    over = lax.broadcasted_iota(jnp.int32, shape, 1)
    earlier, later = over < down, down < over

    def by_row(value):
        return jnp.sum(value, axis=1, keepdims=True)

    def by_column(value):
        return jnp.sum(value, axis=0, keepdims=True)

    def look_up(vector, index):
        column, row = vector
        at_column, at_row = index
        return (
            by_row(jnp.where(over == at_column, row, 0)),
            by_column(jnp.where(down == at_row, column, 0)),
        )

    def last(where, where_t):
        return (
            jnp.max(jnp.where(where, over, -1), axis=1, keepdims=True),
            jnp.max(jnp.where(where_t, down, -1), axis=0, keepdims=True),
        )

    def choose(index, yes, no):
        return tuple(jnp.where(i >= 0, a, b) for i, a, b in zip(index, yes, no))

    p_row = pivots[...]
    p = by_row(jnp.where(down == over, p_row, 0)), p_row
    steps = (
        lax.broadcasted_iota(jnp.int32, (NB, 1), 0), lax.broadcasted_iota(jnp.int32, (1, NB), 1)
    )
    touched = last((p[1] == down) & earlier, (p[0] == over) & later)
    held = choose(touched, touched, steps)
    for _ in range(7):
        held = look_up(held, held)
    same = p[0] == p[1]
    before = last(same & earlier, same & later)
    source = choose(before, look_up(held, before), p)
    owner = tuple(v // rows_dev for v in source)
    alike = owner[0] == owner[1]
    slot = (
        by_row(jnp.where(alike & earlier, 1, 0)), by_column(jnp.where(alike & later, 1, 0))
    )
    offset = source[0] - me * rows_dev
    mine = (owner[0] == me) & (slot[0] == over)
    picked = by_column(jnp.where(mine, offset, 0))
    table[pl.ds(0, 1), pl.ds(0, NB)] = owner[1] * slots + jnp.minimum(slot[1], slots - 1)
    table[pl.ds(1, 1), pl.ds(0, NB)] = picked
    leaves = look_up(held, last(same, same))[0]
    wide = lax.broadcasted_iota(jnp.int32, (NB, PROWS * slots), 1)
    hit = (owner[0] * slots + slot[0] == wide) & (slot[0] < slots)
    table[pl.ds(3, 1), :] = by_column(jnp.where(hit, leaves, 0))
    note[pl.ds(0, 1), :] = picked
    note[pl.ds(1, 1), :] = jnp.broadcast_to(
        by_column(jnp.where(owner[0] == me, 1, 0)), (1, NB)
    )
    most[...] = jnp.broadcast_to(by_row(jnp.max(slot[0], axis=0, keepdims=True)), (1, NB))


def exchange_kernel(
    slots,
    pivots_hbm, matrix,
    resident, gathered, panel, inverse, returned, note, most,
    pivots, table, plan, picks, received, ordered, top, top_a, top_b, back, corner,
    row_send, row_recv, ret_send, ret_recv, ring_send, ring_recv,
    top_send, top_recv, panel_send, panel_recv, low_send, low_recv, own_sem, load_sem,
):
    half = NB // 2
    rows_dev = matrix.shape[0]
    me = lax.axis_index("prow")
    col = lax.axis_index("pcol")
    x, y = me // SIDE, me % SIDE
    z, core = col // 2, col % 2

    def block(q):
        return pl.ds(pl.multiple_of(q * NB, NB), NB)

    def remote(src, dst, send_sem, recv_sem, device):
        return pltpu.make_async_remote_copy(
            src_ref=src, dst_ref=dst, send_sem=send_sem, recv_sem=recv_sem, device_id=device
        )

    def ahead(d):
        return jnp.where(me + d >= PROWS, me + d - PROWS, me + d)

    def behind(d):
        return jnp.where(me >= d, me - d, me - d + PROWS)

    z_up = jnp.where(col >= 6, col - 6, col + 2)
    z_down = jnp.where(col >= 2, col - 2, col + 6)
    other = jnp.where(core == 0, col + 1, col - 1)
    pivots_in = pltpu.make_async_copy(pivots_hbm, pivots, own_sem.at[10])
    pivots_in.start()
    barrier = pltpu.get_barrier_semaphore()
    for d in range(1, PROWS):
        pl.semaphore_signal(barrier, inc=1, device_id={"prow": ahead(d)})
    for c in (z_up, z_down, other):
        pl.semaphore_signal(barrier, inc=1, device_id={"pcol": c})

    @pl.when((me == 0) & (col == 0))
    def _():
        for c in (3, 4, 5, 7):
            pl.semaphore_signal(barrier, inc=1, device_id={"pcol": c})

    far = (col == 3) | (col == 4) | (col == 5) | (col == 7)

    @pl.when((me == 0) & far)
    def _():
        pl.semaphore_signal(barrier, inc=1, device_id={"pcol": 0})

    panel_in = pltpu.make_async_copy(matrix.at[:, pl.ds(0, NB)], panel, own_sem.at[7])

    @pl.when(col == 0)
    def _():
        panel_in.start()

    loads = []
    for k in range(LOADS):
        part = pl.ds(k * (rows_dev // LOADS), rows_dev // LOADS)
        loads.append(
            pltpu.make_async_copy(matrix.at[part, :], resident.at[part, :], load_sem.at[k])
        )
        loads[-1].start()
    extra = jnp.where(me == 0, jnp.where(col == 0, 4, jnp.where(far, 1, 0)), 0)
    pl.semaphore_wait(barrier, PROWS - 1 + 3 + extra)

    def top_x(d):
        return remote(
            resident.at[pl.ds(0, half), pl.ds(d * SIDE * NB, SIDE * NB)], top_a,
            top_send.at[0], top_recv.at[0], {"prow": d * SIDE},
        )

    def top_y(d, k):
        return remote(
            resident.at[pl.ds(half, half), pl.ds((k * SIDE + d) * NB, NB)],
            top_b.at[:, pl.ds(k * NB, NB)],
            top_send.at[0], top_recv.at[1], {"prow": d},
        )

    @pl.when(me == 0)
    def _():
        for c in loads[:1]:
            c.wait()

    def low_copy(k, device):
        return remote(corner, corner, low_send.at[k], low_recv.at[0], device)

    def low_sends_col(act):
        @pl.when((me == 0) & (col == 0))
        def _():
            for c in (4, 5, 2, 6, 3, 7, 1):
                act(low_copy(8 + c, {"pcol": c}))

    def low_sends(act):
        @pl.when(me == 0)
        def _():
            for d in (2, 1, 3):
                act(low_copy(2 + d, {"prow": d * SIDE}))

    def low_sends_y(act):
        @pl.when(y == 0)
        def _():
            for d in (2, 1, 3):
                act(low_copy(5 + d, {"prow": x * SIDE + d}))

    @pl.when((me == 0) & (col == 0))
    def _():
        corner[...] = resident[pl.ds(0, NB), pl.ds(0, NB)]
        low_sends_col(lambda c: c.start())
        low_sends(lambda c: c.start())

    @pl.when(me == 0)
    def _():
        for d in (1, 3, 2):
            top_x(d).start()
            for k in range(SIDE):
                top_y(d, k).start()
        top_a[...] = resident[pl.ds(0, half), pl.ds(0, SIDE * NB)]
        for k in range(SIDE):
            top_b[:, pl.ds(k * NB, NB)] = resident[pl.ds(half, half), pl.ds(k * SIDE * NB, NB)]

    def panel_copy(h, k, to):
        ref = panel.at[pl.ds(pl.multiple_of(h * (rows_dev // 2), 8), rows_dev // 2)]
        return remote(ref, ref, panel_send.at[k], panel_recv.at[h], {"pcol": to})

    @pl.when(col == 0)
    def _():
        panel_in.wait()
        panel_copy(1, 2, other).start()
        panel_copy(0, 0, z_up).start()
        panel_copy(0, 1, z_down).start()
        panel_copy(0, 3, other).start()

    pivots_in.wait()
    swap_plan(slots, pivots, me, rows_dev, table, note, most)
    plan_copy = pltpu.make_async_copy(table, plan, own_sem.at[9])
    plan_copy.start()
    plan_copy.wait()
    @pl.when(me != 0)
    def _():
        for c in loads[:1]:
            c.wait()

    for c in loads[1:]:
        c.wait()

    def pick(g, carry):
        rows = [resident[pl.ds(plan[1, 2 * g + i], 1), :] for i in range(2)]
        for i in range(2):
            for q in range(PROWS):
                picks[pl.ds(q * slots + 2 * g + i, 1), :] = rows[i][:, q * NB : (q + 1) * NB]
        return carry

    lax.fori_loop(0, slots // 2, pick, 0)

    def row_copy(d):
        peer = ahead(d)
        return remote(
            picks.at[pl.ds(pl.multiple_of(peer * slots, 8), slots)],
            received.at[pl.ds(pl.multiple_of(me * slots, 8), slots)],
            row_send.at[0], row_recv.at[0], {"prow": peer},
        )

    def row_all():
        ref = received.at[pl.ds(0, (PROWS - 1) * slots)]
        return remote(ref, ref, row_send.at[0], row_recv.at[0], {"prow": ahead(1)})

    for d in (10, 2, 8, 6, 9, 7, 11, 5, 13, 3, 14, 1, 15, 4, 12):
        row_copy(d).start()

    mine = pl.ds(pl.multiple_of(me * slots, 8), slots)
    received[mine, :] = picks[mine, :]

    @pl.when((me == 0) & (col != 0))
    def _():
        low_copy(0, {"pcol": other}).wait_recv()
        low_sends(lambda c: c.start())

    def panel_leg():
        panel_copy(core, 0, other).wait_recv()

        @pl.when(z > 0)
        def _():
            panel_copy(core, 2, other).start()

        @pl.when((z == 0) | (z == 1 + 2 * core))
        def _():
            panel_copy(core, 0, jnp.where(z == 3, z_down, z_up)).start()

        @pl.when(z == 0)
        def _():
            panel_copy(core, 1, z_down).start()

    def top_leg(a, d):
        if a == 0:
            src, dst, device = top_a, top.at[pl.ds(0, half)], x * SIDE + d
        else:
            src, dst, device = top_b, top.at[pl.ds(half, half)], d * SIDE + y
        return remote(
            src.at[:, pl.ds(d * NB, NB)], dst,
            top_send.at[1 + a], top_recv.at[2 + a], {"prow": device},
        )

    @pl.when(y == 0)
    def _():
        @pl.when(x != 0)
        def _():
            top_x(1).wait_recv()

        for d in range(1, SIDE):
            top_leg(0, d).start()
        top[pl.ds(0, half), :] = top_a[:, pl.ds(0, NB)]

    @pl.when(x == 0)
    def _():
        @pl.when(y != 0)
        def _():
            remote(top_b, top_b, top_send.at[0], top_recv.at[1], {"prow": 1}).wait_recv()

        for d in range(1, SIDE):
            top_leg(1, d).start()
        top[pl.ds(half, half), :] = top_b[:, pl.ds(0, NB)]

    row_all().wait_recv()

    def order(g, carry):
        rows = [received[pl.ds(plan[0, 16 * g + i], 1), :] for i in range(16)]
        for i in range(16):
            ordered[pl.ds(16 * g + i, 1), :] = rows[i]
        return carry

    lax.fori_loop(0, NB // 16, order, 0)
    gathered[:, block(me)] = ordered[...]

    def spot(o, along, across):
        dx, dy = (along, across) if o == 0 else (across, along)
        xx, yy = x + dx, y + dy
        if dx:
            xx = jnp.where(xx >= SIDE, xx - SIDE, jnp.where(xx < 0, xx + SIDE, xx))
        if dy:
            yy = jnp.where(yy >= SIDE, yy - SIDE, jnp.where(yy < 0, yy + SIDE, yy))
        return xx * SIDE + yy

    def ring_copy(o, q, sem, device):
        ref = gathered.at[pl.ds(o * half, half), block(q)]
        return remote(ref, ref, ring_send.at[0], ring_recv.at[sem], {"prow": device})

    def ring_all(blocks, sem):
        ref = gathered.at[:, pl.ds(0, blocks * NB)]
        return remote(ref, ref, ring_send.at[0], ring_recv.at[sem], {"prow": ahead(1)})

    def ring_start(o, q, sem, device):
        ring_copy(o, q, sem, device).start()

    for d in (2, 1, 3):
        for o in (0, 1):
            ring_start(o, me, 2 * d + o - 1, spot(o, d, 0))
    for d in (2, 1, 3):
        for o in (0, 1):
            ring_start(o, me, 0, spot(o, 0, d))

    @pl.when((z != 2) & (col != 0))
    def _():
        panel_leg()

    @pl.when(y == 0)
    def _():
        @pl.when(x != 0)
        def _():
            low_copy(0, {"pcol": other}).wait_recv()

    low_sends_y(lambda c: c.start())

    @pl.when(y != 0)
    def _():
        top_leg(0, 1).wait_recv()

    @pl.when(x != 0)
    def _():
        top_leg(1, 1).wait_recv()

    def back_rows(g, carry):
        rows = [top[pl.ds(plan[3, 16 * g + i], 1), :] for i in range(16)]
        for i in range(16):
            back[pl.ds(16 * g + i, 1), :] = rows[i]
        return carry

    lax.fori_loop(0, PROWS * slots // 16, back_rows, 0)

    def ret_copy(d):
        peer = ahead(d)
        return remote(
            back.at[pl.ds(pl.multiple_of(peer * slots, 8), slots)],
            returned.at[:, block(me)],
            ret_send.at[0], ret_recv.at[0], {"prow": peer},
        )

    def ret_all():
        ref = returned.at[:, pl.ds(0, (PROWS - 1) * NB)]
        return remote(ref, ref, ret_send.at[0], ret_recv.at[0], {"prow": ahead(1)})

    for d in (10, 2, 8, 6, 9, 7, 11, 5, 13, 3, 14, 1, 15, 4, 12):
        ret_copy(d).start()
    ret_own = pltpu.make_async_copy(
        back.at[pl.ds(pl.multiple_of(me * slots, 8), slots)],
        returned.at[:, block(me)], own_sem.at[8],
    )
    ret_own.start()

    for e in (1, 3, 2):
        for o in (0, 1):
            q = spot(o, -e, 0)
            ring_copy(o, q, 2 * e + o - 1, me).wait_recv()
            for d in (2, 1, 3):
                ring_start(o, q, 0, spot(o, 0, d))

    @pl.when(z == 2)
    def _():
        panel_leg()

    @pl.when(y != 0)
    def _():
        low_copy(0, {"pcol": other}).wait_recv()

    inverse[...] = invert_unit_lower(corner[...])

    ring_all(12, 0).wait_recv()
    ret_all().wait_recv()
    ret_own.wait()

    @pl.when(col != 0)
    def _():
        panel_copy(1 - core, 0, other).wait_recv()

    ring_all(15, 0).wait_send()
    row_all().wait_send()
    ret_all().wait_send()

    @pl.when(me == 0)
    def _():
        ref = resident.at[pl.ds(0, NB), pl.ds(0, 12 * NB)]
        remote(ref, ref, top_send.at[0], top_recv.at[0], {"prow": 1}).wait_send()

    @pl.when(y == 0)
    def _():
        ref = top_a.at[:, pl.ds(0, 3 * NB)]
        remote(ref, ref, top_send.at[1], top_recv.at[2], {"prow": 1}).wait_send()

    @pl.when(x == 0)
    def _():
        ref = top_b.at[:, pl.ds(0, 3 * NB)]
        remote(ref, ref, top_send.at[2], top_recv.at[3], {"prow": 1}).wait_send()

    @pl.when(col == 0)
    def _():
        panel_copy(0, 3, other).wait_send()

    @pl.when((z > 0) | (core == 0))
    def _():
        panel_copy(core, 2, other).wait_send()

    @pl.when((z == 0) | (z == 1 + 2 * core))
    def _():
        panel_copy(core, 0, other).wait_send()

    @pl.when(z == 0)
    def _():
        panel_copy(core, 1, other).wait_send()

    low_sends_col(lambda c: c.wait_send())
    low_sends(lambda c: c.wait_send())
    low_sends_y(lambda c: c.wait_send())


def exchange(slots, collective_id, matrix, pivots):
    rows_dev, cols_dev = matrix.shape
    f32, i32 = jnp.float32, jnp.int32
    vmem = pl.BlockSpec(memory_space=pltpu.VMEM)
    hbm = pl.BlockSpec(memory_space=pltpu.HBM)
    dma = pltpu.SemaphoreType.DMA
    return pl.pallas_call(
        functools.partial(exchange_kernel, slots),
        out_shape=[
            pltpu.VMEM((rows_dev, cols_dev), f32),
            jax.ShapeDtypeStruct((NB, cols_dev), f32),
            jax.ShapeDtypeStruct((rows_dev, NB), f32),
            jax.ShapeDtypeStruct((NB, NB), f32),
            jax.ShapeDtypeStruct((slots, cols_dev), f32),
            jax.ShapeDtypeStruct((2, NB), i32),
            jax.ShapeDtypeStruct((1, NB), i32),
        ],
        in_specs=[hbm, hbm],
        out_specs=[vmem] * 7,
        scratch_shapes=[
            pltpu.VMEM((1, NB), i32),
            pltpu.VMEM((8, PROWS * slots), i32),
            pltpu.SMEM((8, PROWS * slots), i32),
            pltpu.VMEM((PROWS * slots, NB), f32),
            pltpu.VMEM((PROWS * slots, NB), f32),
            pltpu.VMEM((NB, NB), f32),
            pltpu.VMEM((NB, NB), f32),
            pltpu.VMEM((NB // 2, SIDE * NB), f32),
            pltpu.VMEM((NB // 2, SIDE * NB), f32),
            pltpu.VMEM((PROWS * slots, NB), f32),
            pltpu.VMEM((NB, NB), f32),
            dma((1,)), dma((1,)), dma((1,)), dma((1,)),
            dma((1,)), dma((7,)),
            dma((3,)), dma((4,)), dma((4,)), dma((2,)), dma((16,)), dma((1,)), dma((11,)),
            dma((LOADS,)),
        ],
        compiler_params=pltpu.CompilerParams(
            collective_id=collective_id, has_side_effects=True, vmem_limit_bytes=24 * MIB
        ),
        name="exchange_%d" % slots,
    )(pivots, pltpu.with_memory_space_constraint(matrix, pltpu.HBM))


def update_kernel(
    note, block, gathered, panel, inverse, returned, out, matrix,
    notes, result, factor, note_sem, sems,
):
    me = lax.axis_index("prow")
    col = lax.axis_index("pcol")
    note_copy = pltpu.make_async_copy(note, notes, note_sem.at[0])
    note_copy.start()
    factor[...] = stacked(panel[...])
    solve = stacked(inverse[...])
    note_copy.wait()

    def replace(s, carry):
        matrix[pl.ds(notes[0, s], 1), :] = returned[pl.ds(s, 1), :]
        return carry

    lax.fori_loop(0, notes[1, 0], replace, 0)

    def write(n):
        return pltpu.make_async_copy(
            result.at[:, pl.ds(n * WIDE, WIDE)], out.at[:, pl.ds(n * WIDE, WIDE)], sems.at[n]
        )

    rows = matrix.shape[0] - NB
    parts = matrix.shape[1] // WIDE
    for n in range(parts):
        here = pl.ds(n * WIDE, WIDE)
        upper = jnp.dot(solve, terms(gathered[:, here]), preferred_element_type=jnp.float32)
        value = matrix[:, here] - jnp.dot(
            factor[...], terms(upper), preferred_element_type=jnp.float32
        )
        head = jnp.where(me == 0, upper, value[:NB])
        if n == 0:
            keep = col == 0
            result[pl.ds(0, NB), pl.ds(0, NB)] = jnp.where(keep, panel[pl.ds(0, NB), :], head[:, :NB])
            result[pl.ds(NB, rows), pl.ds(0, NB)] = jnp.where(
                keep, panel[pl.ds(NB, rows), :], value[NB:, :NB]
            )
            result[pl.ds(0, NB), pl.ds(NB, WIDE - NB)] = head[:, NB:]
            result[pl.ds(NB, rows), pl.ds(NB, WIDE - NB)] = value[NB:, NB:]
        else:
            result[pl.ds(0, NB), here] = head
            result[pl.ds(NB, rows), here] = value[NB:]

        write(n).start()
    for n in range(parts):
        write(n).wait()


def update(matrix, gathered, panel, inverse, returned, note):
    rows_dev, cols_dev = matrix.shape
    vmem = pl.BlockSpec(memory_space=pltpu.VMEM)
    out, _ = pl.pallas_call(
        update_kernel,
        out_shape=[
            pltpu.HBM(matrix.shape, jnp.float32), pltpu.VMEM(matrix.shape, jnp.float32)
        ],
        in_specs=[vmem] * 6,
        out_specs=[pl.BlockSpec(memory_space=pltpu.HBM), vmem],
        input_output_aliases={1: 1},
        scratch_shapes=[
            pltpu.SMEM((2, NB), jnp.int32),
            pltpu.VMEM((rows_dev, cols_dev), jnp.float32),
            pltpu.VMEM((rows_dev, 3 * NB), jnp.bfloat16),
            pltpu.SemaphoreType.DMA((1,)),
            pltpu.SemaphoreType.DMA((cols_dev // WIDE,)),
        ],
        compiler_params=pltpu.CompilerParams(vmem_limit_bytes=28 * MIB),
        name="update",
    )(note, matrix, gathered, panel, inverse, returned)
    return out


def local(matrix, pivots):
    pivots = pivots.reshape(1, NB)
    *found, most = exchange(FEW, 0, matrix, pivots)

    def many():
        *found, _ = exchange(NB, 1, matrix, pivots)
        return update(*found)

    return lax.cond(most[0, 0] < FEW, lambda: update(*found), many)


def solution(mesh):
    placed = (P("prow", "pcol"), P())
    return jax.shard_map(
        local, mesh=mesh, in_specs=placed, out_specs=P("prow", "pcol"), check_vma=False
    )
```

```python
import functools

import jax
import jax.numpy as jnp
from jax import lax
from jax.experimental import pallas as pl
from jax.experimental.pallas import tpu as pltpu
from jax.sharding import PartitionSpec as P

NB = 128
PROWS = 16
SIDE = 4
FEW = 24
MIB = 1024 * 1024
LOADS = 16
WIDE = 256


def split(value):
    high = value.astype(jnp.bfloat16)
    return high, (value - high.astype(jnp.float32)).astype(jnp.bfloat16)


def stacked(value):
    high, low = split(value)
    return jnp.concatenate([high, low, high], axis=1)


def terms(value):
    high, low = split(value)
    return jnp.concatenate([high, high, low], axis=0)


def dot_parts(left, right):
    return jnp.dot(stacked(left), terms(right), preferred_element_type=jnp.float32)


def invert_unit_lower(block):
    rows = lax.broadcasted_iota(jnp.int32, (NB, NB), 0)
    cols = lax.broadcasted_iota(jnp.int32, (NB, NB), 1)
    eye = jnp.where(rows == cols, 1.0, 0.0).astype(jnp.float32)
    inverse = eye
    size = 1
    while size < NB:
        corner = (rows // size == cols // size + 1) & (rows // (2 * size) == cols // (2 * size))
        part = jnp.where(corner, block, 0.0)
        if size == 1:
            inverse = eye - part
        else:
            inverse = inverse - dot_parts(dot_parts(inverse, part), inverse)
        size *= 2
    return inverse


def swap_plan(slots, pivots, me, rows_dev, table, note, most):
    shape = (NB, NB)
    down = lax.broadcasted_iota(jnp.int32, shape, 0)
    over = lax.broadcasted_iota(jnp.int32, shape, 1)
    earlier, later = over < down, down < over

    def by_row(value):
        return jnp.sum(value, axis=1, keepdims=True)

    def by_column(value):
        return jnp.sum(value, axis=0, keepdims=True)

    def look_up(vector, index):
        column, row = vector
        at_column, at_row = index
        return (
            by_row(jnp.where(over == at_column, row, 0)),
            by_column(jnp.where(down == at_row, column, 0)),
        )

    def last(where, where_t):
        return (
            jnp.max(jnp.where(where, over, -1), axis=1, keepdims=True),
            jnp.max(jnp.where(where_t, down, -1), axis=0, keepdims=True),
        )

    def choose(index, yes, no):
        return tuple(jnp.where(i >= 0, a, b) for i, a, b in zip(index, yes, no))

    p_row = pivots[...]
    p = by_row(jnp.where(down == over, p_row, 0)), p_row
    steps = (
        lax.broadcasted_iota(jnp.int32, (NB, 1), 0), lax.broadcasted_iota(jnp.int32, (1, NB), 1)
    )
    touched = last((p[1] == down) & earlier, (p[0] == over) & later)
    held = choose(touched, touched, steps)
    for _ in range(7):
        held = look_up(held, held)
    same = p[0] == p[1]
    before = last(same & earlier, same & later)
    source = choose(before, look_up(held, before), p)
    owner = tuple(v // rows_dev for v in source)
    alike = owner[0] == owner[1]
    slot = (
        by_row(jnp.where(alike & earlier, 1, 0)), by_column(jnp.where(alike & later, 1, 0))
    )
    offset = source[0] - me * rows_dev
    mine = (owner[0] == me) & (slot[0] == over)
    picked = by_column(jnp.where(mine, offset, 0))
    table[pl.ds(0, 1), pl.ds(0, NB)] = owner[1] * slots + jnp.minimum(slot[1], slots - 1)
    table[pl.ds(1, 1), pl.ds(0, NB)] = picked
    leaves = look_up(held, last(same, same))[0]
    wide = lax.broadcasted_iota(jnp.int32, (NB, PROWS * slots), 1)
    hit = (owner[0] * slots + slot[0] == wide) & (slot[0] < slots)
    table[pl.ds(3, 1), :] = by_column(jnp.where(hit, leaves, 0))
    note[pl.ds(0, 1), :] = picked
    note[pl.ds(1, 1), :] = jnp.broadcast_to(
        by_column(jnp.where(owner[0] == me, 1, 0)), (1, NB)
    )
    most[...] = jnp.broadcast_to(by_row(jnp.max(slot[0], axis=0, keepdims=True)), (1, NB))


def exchange_kernel(
    slots,
    pivots_hbm, matrix,
    resident, gathered, panel, inverse, returned, note, most,
    pivots, table, plan, picks, received, ordered, top, top_a, top_b, back, corner,
    row_send, row_recv, ret_send, ret_recv, ring_send, ring_recv,
    top_send, top_recv, panel_send, panel_recv, low_send, low_recv, own_sem, load_sem,
):
    half = NB // 2
    rows_dev = matrix.shape[0]
    me = lax.axis_index("prow")
    col = lax.axis_index("pcol")
    x, y = me // SIDE, me % SIDE
    z, core = col // 2, col % 2

    def block(q):
        return pl.ds(pl.multiple_of(q * NB, NB), NB)

    def remote(src, dst, send_sem, recv_sem, device):
        return pltpu.make_async_remote_copy(
            src_ref=src, dst_ref=dst, send_sem=send_sem, recv_sem=recv_sem, device_id=device
        )

    def ahead(d):
        return jnp.where(me + d >= PROWS, me + d - PROWS, me + d)

    def behind(d):
        return jnp.where(me >= d, me - d, me - d + PROWS)

    z_up = jnp.where(col >= 6, col - 6, col + 2)
    z_down = jnp.where(col >= 2, col - 2, col + 6)
    other = jnp.where(core == 0, col + 1, col - 1)
    pivots_in = pltpu.make_async_copy(pivots_hbm, pivots, own_sem.at[10])
    pivots_in.start()
    barrier = pltpu.get_barrier_semaphore()
    for d in range(1, PROWS):
        pl.semaphore_signal(barrier, inc=1, device_id={"prow": ahead(d)})
    for c in (z_up, z_down, other):
        pl.semaphore_signal(barrier, inc=1, device_id={"pcol": c})

    @pl.when((me == 0) & (col == 0))
    def _():
        for c in (3, 4, 5, 7):
            pl.semaphore_signal(barrier, inc=1, device_id={"pcol": c})

    far = (col == 3) | (col == 4) | (col == 5) | (col == 7)

    @pl.when((me == 0) & far)
    def _():
        pl.semaphore_signal(barrier, inc=1, device_id={"pcol": 0})

    panel_in = pltpu.make_async_copy(matrix.at[:, pl.ds(0, NB)], panel, own_sem.at[7])

    @pl.when(col == 0)
    def _():
        panel_in.start()

    loads = []
    for k in range(LOADS):
        part = pl.ds(k * (rows_dev // LOADS), rows_dev // LOADS)
        loads.append(
            pltpu.make_async_copy(matrix.at[part, :], resident.at[part, :], load_sem.at[k])
        )
        loads[-1].start()
    extra = jnp.where(me == 0, jnp.where(col == 0, 4, jnp.where(far, 1, 0)), 0)
    pl.semaphore_wait(barrier, PROWS - 1 + 3 + extra)

    def top_x(d):
        return remote(
            resident.at[pl.ds(0, half), pl.ds(d * SIDE * NB, SIDE * NB)], top_a,
            top_send.at[0], top_recv.at[0], {"prow": d * SIDE},
        )

    def top_y(d, k):
        return remote(
            resident.at[pl.ds(half, half), pl.ds((k * SIDE + d) * NB, NB)],
            top_b.at[:, pl.ds(k * NB, NB)],
            top_send.at[0], top_recv.at[1], {"prow": d},
        )

    @pl.when(me == 0)
    def _():
        for c in loads[:2]:
            c.wait()

    def low_copy(k, device):
        return remote(corner, corner, low_send.at[k], low_recv.at[0], device)

    def low_sends_col(act):
        @pl.when((me == 0) & (col == 0))
        def _():
            for c in (4, 5, 2, 6, 3, 7, 1):
                act(low_copy(8 + c, {"pcol": c}))

    def low_sends(act):
        @pl.when(me == 0)
        def _():
            for d in (2, 1, 3):
                act(low_copy(2 + d, {"prow": d * SIDE}))

    def low_sends_y(act):
        @pl.when(y == 0)
        def _():
            for d in (2, 1, 3):
                act(low_copy(5 + d, {"prow": x * SIDE + d}))

    @pl.when((me == 0) & (col == 0))
    def _():
        corner[...] = resident[pl.ds(0, NB), pl.ds(0, NB)]
        low_sends_col(lambda c: c.start())
        low_sends(lambda c: c.start())

    @pl.when(me == 0)
    def _():
        for d in (1, 3, 2):
            top_x(d).start()
            for k in range(SIDE):
                top_y(d, k).start()
        top_a[...] = resident[pl.ds(0, half), pl.ds(0, SIDE * NB)]
        for k in range(SIDE):
            top_b[:, pl.ds(k * NB, NB)] = resident[pl.ds(half, half), pl.ds(k * SIDE * NB, NB)]

    def panel_copy(h, k, to):
        ref = panel.at[pl.ds(pl.multiple_of(h * (rows_dev // 2), 8), rows_dev // 2)]
        return remote(ref, ref, panel_send.at[k], panel_recv.at[h], {"pcol": to})

    @pl.when(col == 0)
    def _():
        panel_in.wait()
        panel_copy(1, 2, other).start()
        panel_copy(0, 0, z_up).start()
        panel_copy(0, 1, z_down).start()
        panel_copy(0, 3, other).start()

    pivots_in.wait()
    swap_plan(slots, pivots, me, rows_dev, table, note, most)
    plan_copy = pltpu.make_async_copy(table, plan, own_sem.at[9])
    plan_copy.start()
    plan_copy.wait()
    @pl.when(me != 0)
    def _():
        for c in loads[:2]:
            c.wait()

    for c in loads[2:]:
        c.wait()

    def pick(g, carry):
        rows = [resident[pl.ds(plan[1, 2 * g + i], 1), :] for i in range(2)]
        for i in range(2):
            for q in range(PROWS):
                picks[pl.ds(q * slots + 2 * g + i, 1), :] = rows[i][:, q * NB : (q + 1) * NB]
        return carry

    lax.fori_loop(0, slots // 2, pick, 0)

    def row_copy(d):
        peer = ahead(d)
        return remote(
            picks.at[pl.ds(pl.multiple_of(peer * slots, 8), slots)],
            received.at[pl.ds(pl.multiple_of(me * slots, 8), slots)],
            row_send.at[0], row_recv.at[0], {"prow": peer},
        )

    def row_all():
        ref = received.at[pl.ds(0, (PROWS - 1) * slots)]
        return remote(ref, ref, row_send.at[0], row_recv.at[0], {"prow": ahead(1)})

    for d in (10, 2, 8, 6, 9, 7, 11, 5, 13, 3, 14, 1, 15, 4, 12):
        row_copy(d).start()

    mine = pl.ds(pl.multiple_of(me * slots, 8), slots)
    received[mine, :] = picks[mine, :]

    @pl.when((me == 0) & (col != 0))
    def _():
        low_copy(0, {"pcol": other}).wait_recv()
        low_sends(lambda c: c.start())

    def panel_leg():
        panel_copy(core, 0, other).wait_recv()

        @pl.when(z > 0)
        def _():
            panel_copy(core, 2, other).start()

        @pl.when((z == 0) | (z == 1 + 2 * core))
        def _():
            panel_copy(core, 0, jnp.where(z == 3, z_down, z_up)).start()

        @pl.when(z == 0)
        def _():
            panel_copy(core, 1, z_down).start()

    def top_leg(a, d):
        if a == 0:
            src, dst, device = top_a, top.at[pl.ds(0, half)], x * SIDE + d
        else:
            src, dst, device = top_b, top.at[pl.ds(half, half)], d * SIDE + y
        return remote(
            src.at[:, pl.ds(d * NB, NB)], dst,
            top_send.at[1 + a], top_recv.at[2 + a], {"prow": device},
        )

    @pl.when(y == 0)
    def _():
        @pl.when(x != 0)
        def _():
            top_x(1).wait_recv()

        for d in range(1, SIDE):
            top_leg(0, d).start()
        top[pl.ds(0, half), :] = top_a[:, pl.ds(0, NB)]

    @pl.when(x == 0)
    def _():
        @pl.when(y != 0)
        def _():
            remote(top_b, top_b, top_send.at[0], top_recv.at[1], {"prow": 1}).wait_recv()

        for d in range(1, SIDE):
            top_leg(1, d).start()
        top[pl.ds(half, half), :] = top_b[:, pl.ds(0, NB)]

    row_all().wait_recv()

    def order(g, carry):
        rows = [received[pl.ds(plan[0, 16 * g + i], 1), :] for i in range(16)]
        for i in range(16):
            ordered[pl.ds(16 * g + i, 1), :] = rows[i]
        return carry

    lax.fori_loop(0, NB // 16, order, 0)
    gathered[:, block(me)] = ordered[...]

    def spot(o, along, across):
        dx, dy = (along, across) if o == 0 else (across, along)
        xx, yy = x + dx, y + dy
        if dx:
            xx = jnp.where(xx >= SIDE, xx - SIDE, jnp.where(xx < 0, xx + SIDE, xx))
        if dy:
            yy = jnp.where(yy >= SIDE, yy - SIDE, jnp.where(yy < 0, yy + SIDE, yy))
        return xx * SIDE + yy

    def ring_copy(o, q, sem, device):
        ref = gathered.at[pl.ds(o * half, half), block(q)]
        return remote(ref, ref, ring_send.at[0], ring_recv.at[sem], {"prow": device})

    def ring_all(blocks, sem):
        ref = gathered.at[:, pl.ds(0, blocks * NB)]
        return remote(ref, ref, ring_send.at[0], ring_recv.at[sem], {"prow": ahead(1)})

    def ring_start(o, q, sem, device):
        ring_copy(o, q, sem, device).start()

    for d in (2, 1, 3):
        for o in (0, 1):
            ring_start(o, me, 2 * d + o - 1, spot(o, d, 0))
    for d in (2, 1, 3):
        for o in (0, 1):
            ring_start(o, me, 0, spot(o, 0, d))

    @pl.when((z != 2) & (col != 0))
    def _():
        panel_leg()

    @pl.when(y == 0)
    def _():
        @pl.when(x != 0)
        def _():
            low_copy(0, {"pcol": other}).wait_recv()

    low_sends_y(lambda c: c.start())

    @pl.when(y != 0)
    def _():
        top_leg(0, 1).wait_recv()

    @pl.when(x != 0)
    def _():
        top_leg(1, 1).wait_recv()

    def back_rows(g, carry):
        rows = [top[pl.ds(plan[3, 16 * g + i], 1), :] for i in range(16)]
        for i in range(16):
            back[pl.ds(16 * g + i, 1), :] = rows[i]
        return carry

    lax.fori_loop(0, PROWS * slots // 16, back_rows, 0)

    def ret_copy(d):
        peer = ahead(d)
        return remote(
            back.at[pl.ds(pl.multiple_of(peer * slots, 8), slots)],
            returned.at[:, block(me)],
            ret_send.at[0], ret_recv.at[0], {"prow": peer},
        )

    def ret_all():
        ref = returned.at[:, pl.ds(0, (PROWS - 1) * NB)]
        return remote(ref, ref, ret_send.at[0], ret_recv.at[0], {"prow": ahead(1)})

    for d in (10, 2, 8, 6, 9, 7, 11, 5, 13, 3, 14, 1, 15, 4, 12):
        ret_copy(d).start()
    ret_own = pltpu.make_async_copy(
        back.at[pl.ds(pl.multiple_of(me * slots, 8), slots)],
        returned.at[:, block(me)], own_sem.at[8],
    )
    ret_own.start()

    for e in (1, 3, 2):
        for o in (0, 1):
            q = spot(o, -e, 0)
            ring_copy(o, q, 2 * e + o - 1, me).wait_recv()
            for d in (2, 1, 3):
                ring_start(o, q, 0, spot(o, 0, d))

    @pl.when(z == 2)
    def _():
        panel_leg()

    @pl.when(y != 0)
    def _():
        low_copy(0, {"pcol": other}).wait_recv()

    inverse[...] = invert_unit_lower(corner[...])

    ring_all(12, 0).wait_recv()
    ret_all().wait_recv()
    ret_own.wait()

    @pl.when(col != 0)
    def _():
        panel_copy(1 - core, 0, other).wait_recv()

    ring_all(15, 0).wait_send()
    row_all().wait_send()
    ret_all().wait_send()

    @pl.when(me == 0)
    def _():
        ref = resident.at[pl.ds(0, NB), pl.ds(0, 12 * NB)]
        remote(ref, ref, top_send.at[0], top_recv.at[0], {"prow": 1}).wait_send()

    @pl.when(y == 0)
    def _():
        ref = top_a.at[:, pl.ds(0, 3 * NB)]
        remote(ref, ref, top_send.at[1], top_recv.at[2], {"prow": 1}).wait_send()

    @pl.when(x == 0)
    def _():
        ref = top_b.at[:, pl.ds(0, 3 * NB)]
        remote(ref, ref, top_send.at[2], top_recv.at[3], {"prow": 1}).wait_send()

    @pl.when(col == 0)
    def _():
        panel_copy(0, 3, other).wait_send()

    @pl.when((z > 0) | (core == 0))
    def _():
        panel_copy(core, 2, other).wait_send()

    @pl.when((z == 0) | (z == 1 + 2 * core))
    def _():
        panel_copy(core, 0, other).wait_send()

    @pl.when(z == 0)
    def _():
        panel_copy(core, 1, other).wait_send()

    low_sends_col(lambda c: c.wait_send())
    low_sends(lambda c: c.wait_send())
    low_sends_y(lambda c: c.wait_send())


def exchange(slots, collective_id, matrix, pivots):
    rows_dev, cols_dev = matrix.shape
    f32, i32 = jnp.float32, jnp.int32
    vmem = pl.BlockSpec(memory_space=pltpu.VMEM)
    hbm = pl.BlockSpec(memory_space=pltpu.HBM)
    dma = pltpu.SemaphoreType.DMA
    return pl.pallas_call(
        functools.partial(exchange_kernel, slots),
        out_shape=[
            pltpu.VMEM((rows_dev, cols_dev), f32),
            jax.ShapeDtypeStruct((NB, cols_dev), f32),
            jax.ShapeDtypeStruct((rows_dev, NB), f32),
            jax.ShapeDtypeStruct((NB, NB), f32),
            jax.ShapeDtypeStruct((slots, cols_dev), f32),
            jax.ShapeDtypeStruct((2, NB), i32),
            jax.ShapeDtypeStruct((1, NB), i32),
        ],
        in_specs=[hbm, hbm],
        out_specs=[vmem] * 7,
        scratch_shapes=[
            pltpu.VMEM((1, NB), i32),
            pltpu.VMEM((8, PROWS * slots), i32),
            pltpu.SMEM((8, PROWS * slots), i32),
            pltpu.VMEM((PROWS * slots, NB), f32),
            pltpu.VMEM((PROWS * slots, NB), f32),
            pltpu.VMEM((NB, NB), f32),
            pltpu.VMEM((NB, NB), f32),
            pltpu.VMEM((NB // 2, SIDE * NB), f32),
            pltpu.VMEM((NB // 2, SIDE * NB), f32),
            pltpu.VMEM((PROWS * slots, NB), f32),
            pltpu.VMEM((NB, NB), f32),
            dma((1,)), dma((1,)), dma((1,)), dma((1,)),
            dma((1,)), dma((7,)),
            dma((3,)), dma((4,)), dma((4,)), dma((2,)), dma((16,)), dma((1,)), dma((11,)),
            dma((LOADS,)),
        ],
        compiler_params=pltpu.CompilerParams(
            collective_id=collective_id, has_side_effects=True, vmem_limit_bytes=24 * MIB
        ),
        name="exchange_%d" % slots,
    )(pivots, pltpu.with_memory_space_constraint(matrix, pltpu.HBM))


def update_kernel(
    note, block, gathered, panel, inverse, returned, out, matrix,
    notes, result, factor, note_sem, sems,
):
    me = lax.axis_index("prow")
    col = lax.axis_index("pcol")
    note_copy = pltpu.make_async_copy(note, notes, note_sem.at[0])
    note_copy.start()
    factor[...] = stacked(panel[...])
    solve = stacked(inverse[...])
    note_copy.wait()

    def replace(s, carry):
        matrix[pl.ds(notes[0, s], 1), :] = returned[pl.ds(s, 1), :]
        return carry

    lax.fori_loop(0, notes[1, 0], replace, 0)

    def write(n):
        return pltpu.make_async_copy(
            result.at[:, pl.ds(n * WIDE, WIDE)], out.at[:, pl.ds(n * WIDE, WIDE)], sems.at[n]
        )

    rows = matrix.shape[0] - NB
    parts = matrix.shape[1] // WIDE
    for n in range(parts):
        here = pl.ds(n * WIDE, WIDE)
        upper = jnp.dot(solve, terms(gathered[:, here]), preferred_element_type=jnp.float32)
        value = matrix[:, here] - jnp.dot(
            factor[...], terms(upper), preferred_element_type=jnp.float32
        )
        head = jnp.where(me == 0, upper, value[:NB])
        if n == 0:
            keep = col == 0
            result[pl.ds(0, NB), pl.ds(0, NB)] = jnp.where(keep, panel[pl.ds(0, NB), :], head[:, :NB])
            result[pl.ds(NB, rows), pl.ds(0, NB)] = jnp.where(
                keep, panel[pl.ds(NB, rows), :], value[NB:, :NB]
            )
            result[pl.ds(0, NB), pl.ds(NB, WIDE - NB)] = head[:, NB:]
            result[pl.ds(NB, rows), pl.ds(NB, WIDE - NB)] = value[NB:, NB:]
        else:
            result[pl.ds(0, NB), here] = head
            result[pl.ds(NB, rows), here] = value[NB:]

        write(n).start()
    for n in range(parts):
        write(n).wait()


def update(matrix, gathered, panel, inverse, returned, note):
    rows_dev, cols_dev = matrix.shape
    vmem = pl.BlockSpec(memory_space=pltpu.VMEM)
    out, _ = pl.pallas_call(
        update_kernel,
        out_shape=[
            pltpu.HBM(matrix.shape, jnp.float32), pltpu.VMEM(matrix.shape, jnp.float32)
        ],
        in_specs=[vmem] * 6,
        out_specs=[pl.BlockSpec(memory_space=pltpu.HBM), vmem],
        input_output_aliases={1: 1},
        scratch_shapes=[
            pltpu.SMEM((2, NB), jnp.int32),
            pltpu.VMEM((rows_dev, cols_dev), jnp.float32),
            pltpu.VMEM((rows_dev, 3 * NB), jnp.bfloat16),
            pltpu.SemaphoreType.DMA((1,)),
            pltpu.SemaphoreType.DMA((cols_dev // WIDE,)),
        ],
        compiler_params=pltpu.CompilerParams(vmem_limit_bytes=28 * MIB),
        name="update",
    )(note, matrix, gathered, panel, inverse, returned)
    return out


def local(matrix, pivots):
    pivots = pivots.reshape(1, NB)
    *found, most = exchange(FEW, 0, matrix, pivots)

    def many():
        *found, _ = exchange(NB, 1, matrix, pivots)
        return update(*found)

    return lax.cond(most[0, 0] < FEW, lambda: update(*found), many)


def solution(mesh):
    placed = (P("prow", "pcol"), P())
    return jax.shard_map(
        local, mesh=mesh, in_specs=placed, out_specs=P("prow", "pcol"), check_vma=False
    )
```
